512 devices in a mesh: tensor: 128 (over z, y_lo, x, core), dp: 4 (over y_hi).
Axes of the slice: x: 4, y: 8 (y_hi: 4, y_lo: 2; y = y_hi * 2 + y_lo), z: 8, core: 2. Of those that a mesh axis runs over, the one named last changes fastest.
Arguments:
- tokens: bfloat16 [1024, 4096], P(('dp', 'tensor')), parts along dimension 0, may hold values from -120 to 120
- gate_weight: bfloat16 [26624, 4096], P('tensor'), may hold values from -0.09375 to 0.09375
- up_weight: bfloat16 [26624, 4096], P('tensor'), may hold values from -0.09375 to 0.09375
- down_weight: bfloat16 [26624, 4096], P('tensor'), may hold values from -0.0390625 to 0.0390625
Outputs:
- output: bfloat16 [1024, 4096], P(('dp', 'tensor')), parts along dimension 0
The draws below stay inside these ranges and needn't reach their ends.
There are 4 independent parts, one for each index of `dp`. The reference program is written for one: setup_inputs(seed, part) draws one part's arguments, and reference() takes and returns one part's arrays. A program takes and returns all parts, laid end to end along the dimension named above; an argument that names none is the same for every part. Nothing has to cross between parts.
All inputs are finite; a program needn't handle non-finite values. Where the reference program divides by a largest or mean magnitude, that divisor is 1e-20 or more.
Results may differ from the reference program's by a relative error of at most 0.0065.
Values may be sent and summed in bfloat16 or wider, within the bound.
A program may use at most 64 MiB of HBM per device.

```python
import math
import jax
import jax.numpy as jnp
from jax import lax

D = 4096
FF = 26624
TOKENS = 256


def draw_tokens(key, part):
    key = jax.random.fold_in(key, 7)
    first_key, second_key, third_key = jax.random.split(key, 3)
    values = jnp.clip(jax.random.normal(first_key, (TOKENS, D), jnp.float32), -6.0, 6.0)
    spread = math.log(10.0)
    row_scale = jnp.exp(jax.random.uniform(second_key, (TOKENS, 1), jnp.float32, 0.0, spread))
    overall = jnp.exp(jax.random.uniform(third_key, (), jnp.float32, math.log(0.5), math.log(2.0)))
    return (values * row_scale * overall).astype(jnp.bfloat16)


def shard_levels(rng, extent, cuts, smallest, high):
    level = 1.0
    for dim, blocks in cuts:
        heights = jax.random.uniform(jax.random.fold_in(jax.random.fold_in(rng, 6), dim), (blocks,), jnp.float32, smallest / len(cuts), high / len(cuts))
        level = level * jnp.repeat(jnp.exp(heights), extent[dim] // blocks).reshape((-1,) + (1,) * (len(extent) - 1 - dim))
    return level


def normal_values(stream_key, extent, scale, limit, cuts=(), kind=jnp.bfloat16):
    result = scale * jax.random.normal(stream_key, extent, jnp.float32)
    if cuts:
        result = result * shard_levels(stream_key, extent, cuts, -0.22, 0.18)
    return jnp.clip(result, -limit, limit).astype(kind)


def setup_inputs(seed: int = 0, part: int = 0) -> dict:
    streams_of = jax.random.split(jax.random.key(seed), 5)
    part_splits = jax.random.split(jax.random.fold_in(streams_of[4], part), 5)
    return {
        "tokens": draw_tokens(jax.random.fold_in(jax.random.fold_in(streams_of[4], part), 71), part),
        "gate_weight": normal_values(streams_of[1], (FF, D), D ** -0.5, 0.09375, ((0, 128),)),
        "up_weight": normal_values(streams_of[2], (FF, D), D ** -0.5, 0.09375, ((0, 128),)),
        "down_weight": normal_values(streams_of[3], (FF, D), FF ** -0.5, 0.0390625, ((0, 128),)),
    }


TARGET = 16.0
EPSILON = 1e-6


def by_rows(left, weight):
    return lax.dot_general(left, weight, (((1,), (1,)), ((), ())), preferred_element_type=jnp.float32)


def reference(tokens, gate_weight, up_weight, down_weight):
    wide = tokens.astype(jnp.float32)
    peak = jnp.max(jnp.abs(wide))
    factor = TARGET / (peak + EPSILON)
    scaled = (wide * factor).astype(jnp.bfloat16)
    gate = by_rows(scaled, gate_weight)
    upward = by_rows(scaled, up_weight)
    hidden = (jax.nn.silu(gate) * upward).astype(jnp.bfloat16)
    return jnp.dot(hidden, down_weight, preferred_element_type=jnp.float32).astype(jnp.bfloat16)
```

```python
import jax
import jax.numpy as jnp
from jax import lax
from jax.experimental import pallas as pl
from jax.experimental.pallas import tpu as pltpu
from jax.sharding import PartitionSpec as P

TARGET = 16.0
EPSILON = 1e-06
F32, BF16 = jnp.float32, jnp.bfloat16

D = 4096
UNITS = 208
NZ, NX, NY = 8, 4, 2
NXY = NX * NY
CHIPS = NZ * NXY
LANES = 128
NJ = D // LANES
ROWS = 2 * NJ
CUT = 16
NEAR = (0, 1, 7, 2, 6, 3, 5, 4)
FAR = (4, 3, 5, 2, 6, 1, 7, 0)


def kernel(
    x_ref, wg_ref, wu_ref, wd_ref, o_ref,
    rx, fx, xs, wg, wu, wd, gacc, uacc, part, sums, sb, ra4, ra1, sb4, sb1, rb4, rb1, tmp, pk,
    load_sem, wsend, wrecv, pk_sem,
    ag_send, ag4_z, ag1_p, ag4_p, ag1_z,
    rs_send, rs4_p, rs1_z, rs4_z, rs1_p,
):
    me = lax.axis_index("tensor")
    core = lax.rem(me, 2)
    chip = me // 2
    z, xy = chip // NXY, lax.rem(chip, NXY)
    y, x = xy // NX, lax.rem(xy, NX)

    def plane(k):
        return lax.rem(y + k // NX, NY) * NX + lax.rem(x + lax.rem(k, NX), NX)

    def zed(k):
        return lax.rem(z + k, NZ)

    def dev(zz, pp):
        return {"tensor": (zz * NXY + pp) * 2 + core}

    sibling = {"tensor": chip * 2 + 1 - core}

    def send(src, dst, ssem, rsem, to):
        pltpu.make_async_remote_copy(src, dst, ssem, rsem, device_id=to, device_id_type=pl.DeviceIdType.MESH).start()

    def arrive(ref, sem):
        pltpu.make_async_copy(ref, ref, sem).wait()

    barrier = pltpu.get_barrier_semaphore()

    def greet(k, _):
        pl.semaphore_signal(barrier, inc=1, device_id=dev(zed(k), xy), device_id_type=pl.DeviceIdType.MESH)
        pl.semaphore_signal(barrier, inc=1, device_id=dev(z, plane(k)), device_id_type=pl.DeviceIdType.MESH)
        return 0

    lax.fori_loop(1, 8, greet, 0)
    pl.semaphore_signal(barrier, inc=1, device_id=sibling, device_id_type=pl.DeviceIdType.MESH)

    own = [(wg_ref, wg), (wu_ref, wu), (wd_ref, wd)]
    for i, (src, dst) in enumerate(own):
        pltpu.make_async_copy(src, dst.at[pl.ds(0, UNITS)], load_sem.at[i]).start()

    mine = x_ref[...].astype(F32)
    for j in range(NJ):
        tmp[2 * j : 2 * j + 2, :] = mine[:, j * LANES : (j + 1) * LANES]
    rx[chip] = tmp[...].astype(BF16)

    pl.semaphore_wait(barrier, 15)

    low, high = pl.ds(0, CUT), pl.ds(CUT, ROWS - CUT)

    def first(k, _):
        send(rx.at[chip, high], rx.at[chip, high], ag_send.at[0], ag4_z.at[k], dev(zed(k), xy))
        send(rx.at[chip, low], rx.at[chip, low], ag_send.at[1], ag1_p.at[k], dev(z, plane(k)))
        return 0

    lax.fori_loop(1, 8, first, 0)

    def spread(i):
        block = zed(NEAR[i]) * NXY + xy
        if NEAR[i]:
            arrive(rx.at[block, high], ag4_z.at[NZ - NEAR[i]])

        def to_plane(k, _):
            send(rx.at[block, high], rx.at[block, high], ag_send.at[2], ag4_p.at[i], dev(z, plane(k)))
            return 0

        lax.fori_loop(1, 8, to_plane, 0)

    spread(0)
    for i, (src, dst) in enumerate(own):
        send(src, dst.at[pl.ds(UNITS, UNITS)], wsend.at[i], wrecv.at[i], sibling)
    spread(1)
    spread(2)

    def hear(k, _):
        arrive(rx.at[0, low], ag1_p.at[k])
        return 0

    lax.fori_loop(1, 8, hear, 0)

    def to_z(k, _):
        blocks = rx.at[pl.ds(z * NXY, NXY), low]
        send(blocks, blocks, ag_send.at[3], ag1_z.at[k], dev(zed(k), xy))
        return 0

    lax.fori_loop(1, 8, to_z, 0)
    for i in range(3, NZ):
        spread(i)

    peak = jnp.zeros((8, LANES), F32)
    for i in range(NZ):
        zz = zed(NEAR[i])
        arrive(rx.at[pl.ds(0, 7), high], ag4_p.at[i])
        if NEAR[i]:
            arrive(rx.at[pl.ds(0, NXY), low], ag1_z.at[NZ - NEAR[i]])
        for b in range(NXY):
            wide = rx[zz * NXY + b].astype(F32)
            fx[b * ROWS : (b + 1) * ROWS, :] = wide
            peak = jnp.maximum(peak, jnp.max(jnp.abs(wide).reshape(ROWS // 8, 8, LANES), axis=0))
        for j in range(NJ):
            pair = [fx[pl.ds(2 * j + t, 8, stride=ROWS), :] for t in range(2)]
            xs[pl.ds(pl.multiple_of(zz * 16, 16), 16), j * LANES : (j + 1) * LANES] = jnp.concatenate(pair, axis=0).astype(BF16)

    pk[0] = peak
    peak_copy = pltpu.make_async_remote_copy(
        pk.at[0], pk.at[1], pk_sem.at[0], pk_sem.at[1], device_id=sibling, device_id_type=pl.DeviceIdType.MESH
    )
    peak_copy.start()

    for i, (src, dst) in enumerate(own[:2]):
        pltpu.make_async_copy(src, dst.at[pl.ds(0, UNITS)], load_sem.at[i]).wait()
        arrive(dst.at[pl.ds(UNITS, UNITS)], wrecv.at[i])

    DEPTH = 512
    gacc[...] = jnp.zeros_like(gacc)
    uacc[...] = jnp.zeros_like(uacc)

    def contract(s, _):
        cols = pl.ds(pl.multiple_of(s * DEPTH, DEPTH), DEPTH)
        left = xs[:, cols]
        dims = (((1,), (1,)), ((), ()))
        gacc[...] += lax.dot_general(left, wg[:, cols], dims, preferred_element_type=F32)
        uacc[...] += lax.dot_general(left, wu[:, cols], dims, preferred_element_type=F32)
        return 0

    lax.fori_loop(0, D // DEPTH, contract, 0)

    peak_copy.wait()
    top = jnp.max(jnp.maximum(peak, pk[1]), keepdims=True)
    factor = TARGET / (top + EPSILON)
    gate = gacc[...] * factor
    hidden = (gate / (1.0 + jnp.exp(-gate)) * (uacc[...] * factor)).astype(BF16)

    pltpu.make_async_copy(wd_ref, wd.at[pl.ds(0, UNITS)], load_sem.at[2]).wait()
    arrive(wd.at[pl.ds(UNITS, UNITS)], wrecv.at[2])
    WIDTH = 512

    def expand(s, _):
        cols = pl.ds(pl.multiple_of(s * WIDTH, WIDTH), WIDTH)
        part[:, cols] = jnp.dot(hidden, wd[:, cols], preferred_element_type=F32)
        return 0

    lax.fori_loop(0, D // WIDTH, expand, 0)

    for i in range(NZ):
        zz = zed(FAR[i])
        for j in range(NJ):
            for t in range(2):
                rows = part[pl.ds(pl.multiple_of(zz * 16 + t * 8, 8), 8), j * LANES : (j + 1) * LANES]
                sums[pl.ds(zz * (NXY * ROWS) + 2 * j + t, 8, stride=ROWS), :] = rows
        for b in range(NXY):
            sb[zz * NXY + b] = sums[pl.ds(pl.multiple_of((zz * NXY + b) * ROWS, ROWS), ROWS), :].astype(BF16)

        def to_plane(k, _):
            send(sb.at[zz * NXY + plane(k), high], ra4.at[i, k - 1], rs_send.at[0], rs4_p.at[i], dev(z, plane(k)))
            return 0

        lax.fori_loop(1, 8, to_plane, 0)
        if FAR[i]:
            send(sb.at[pl.ds(zz * NXY, NXY), low], ra1.at[i], rs_send.at[1], rs1_z.at[i], dev(zz, xy))

    def mine_of(block, start, size):
        return sums[pl.ds(pl.multiple_of(block * ROWS + start, 16), size), :]

    def gather4(i):
        zz = zed(FAR[i])
        arrive(ra4.at[i], rs4_p.at[i])
        total = mine_of(zz * NXY + xy, CUT, ROWS - CUT)
        for k in range(7):
            total = total + ra4[i, k].astype(F32)
        if FAR[i]:
            sb4[i] = total.astype(BF16)
            send(sb4.at[i], rb4.at[i], rs_send.at[2], rs4_z.at[i], dev(zz, xy))
        else:
            tmp[CUT:, :] = total

    def gather1():
        for i in range(7):
            arrive(ra1.at[i], rs1_z.at[i])

        def one(k, _):
            p = plane(k)
            total = mine_of(z * NXY + p, 0, CUT)
            for i in range(7):
                total = total + ra1[i, p].astype(F32)
            sb1[k] = total.astype(BF16)
            send(sb1.at[k], rb1.at[k], rs_send.at[3], rs1_p.at[k], dev(z, p))
            return 0

        lax.fori_loop(1, 8, one, 0)
        total = mine_of(chip, 0, CUT)
        for i in range(7):
            total = total + ra1[i, xy].astype(F32)
        tmp[:CUT, :] = total

    for i in range(NZ):
        gather4(i)
    gather1()

    for i in range(7):
        arrive(rb4.at[i], rs4_z.at[i])
        tmp[CUT:, :] += rb4[i].astype(F32)
    for k in range(1, 8):
        arrive(rb1.at[k], rs1_p.at[k])
        tmp[:CUT, :] += rb1[k].astype(F32)
    for j in range(NJ):
        o_ref[:, j * LANES : (j + 1) * LANES] = tmp[2 * j : 2 * j + 2, :].astype(BF16)

    for i, (src, dst) in enumerate(own):
        arrive(dst.at[pl.ds(UNITS, UNITS)], wsend.at[i])
    arrive(rx.at[pl.ds(0, 7), high], ag_send.at[0])
    arrive(rx.at[pl.ds(0, 7), low], ag_send.at[1])
    arrive(rx.at[pl.ds(0, 56), high], ag_send.at[2])
    arrive(rx.at[pl.ds(0, 56), low], ag_send.at[3])
    arrive(sb.at[pl.ds(0, 56), high], rs_send.at[0])
    arrive(sb.at[pl.ds(0, 56), low], rs_send.at[1])
    arrive(sb.at[pl.ds(0, 7), high], rs_send.at[2])
    arrive(sb.at[pl.ds(0, 7), low], rs_send.at[3])


def shards(tokens, gate_weight, up_weight, down_weight):
    vmem, hbm = pl.BlockSpec(memory_space=pltpu.VMEM), pl.BlockSpec(memory_space=pl.ANY)
    dma = pltpu.SemaphoreType.DMA
    high = ROWS - CUT
    return pl.pallas_call(
        kernel,
        out_shape=jax.ShapeDtypeStruct((2, D), BF16),
        in_specs=[vmem, hbm, hbm, hbm],
        out_specs=vmem,
        scratch_shapes=[
            pltpu.VMEM((CHIPS, ROWS, LANES), BF16),
            pltpu.VMEM((NXY * ROWS, LANES), F32),
            pltpu.VMEM((2 * CHIPS, D), BF16),
            pltpu.VMEM((2 * UNITS, D), BF16),
            pltpu.VMEM((2 * UNITS, D), BF16),
            pltpu.VMEM((2 * UNITS, D), BF16),
            pltpu.VMEM((2 * CHIPS, 2 * UNITS), F32),
            pltpu.VMEM((2 * CHIPS, 2 * UNITS), F32),
            pltpu.VMEM((2 * CHIPS, D), F32),
            pltpu.VMEM((CHIPS * ROWS, LANES), F32),
            pltpu.VMEM((CHIPS, ROWS, LANES), BF16),
            pltpu.VMEM((NZ, 7, high, LANES), BF16),
            pltpu.VMEM((7, NXY, CUT, LANES), BF16),
            pltpu.VMEM((7, high, LANES), BF16),
            pltpu.VMEM((8, CUT, LANES), BF16),
            pltpu.VMEM((7, high, LANES), BF16),
            pltpu.VMEM((8, CUT, LANES), BF16),
            pltpu.VMEM((ROWS, LANES), F32),
            pltpu.VMEM((2, 8, LANES), F32),
            dma((3,)), dma((3,)), dma((3,)), dma((2,)),
            dma((4,)), dma((8,)), dma((8,)), dma((8,)), dma((8,)),
            dma((4,)), dma((8,)), dma((7,)), dma((7,)), dma((8,)),
        ],
        compiler_params=pltpu.CompilerParams(collective_id=0, has_side_effects=True, vmem_limit_bytes=48 << 20),
        name="ffn",
    )(tokens, gate_weight, up_weight, down_weight)


def solution(mesh):
    placed = (P(("dp", "tensor"), None), P("tensor", None), P("tensor", None), P("tensor", None))
    return jax.shard_map(
        shards, mesh=mesh, in_specs=placed, out_specs=P(("dp", "tensor"), None), check_vma=False
    )
```

```python
import jax
import jax.numpy as jnp
from jax import lax
from jax.experimental import pallas as pl
from jax.experimental.pallas import tpu as pltpu
from jax.sharding import PartitionSpec as P

TARGET = 16.0
EPSILON = 1e-06
F32, BF16 = jnp.float32, jnp.bfloat16

D = 4096
UNITS = 208
NZ, NX, NY = 8, 4, 2
NXY = NX * NY
CHIPS = NZ * NXY
LANES = 128
NJ = D // LANES
ROWS = 2 * NJ
CUT = 16
NEAR = (0, 1, 7, 2, 6, 3, 5, 4)
FAR = (4, 3, 5, 2, 6, 1, 7, 0)
FAR_PLANE = (6, 5, 7, 2, 4, 1, 3)


def kernel(
    x_ref, wg_ref, wu_ref, wd_ref, o_ref,
    x_in, rx, fx, xs, wg, wu, wd, part, sums, sb, ra4, ra1, sb4, sb1, rb4, rb1, tmp, pk,
    x_sem, load_sem, wsend, wrecv, pk_sem,
    ag_send, ag4_z, ag1_p, ag4_p, ag1_z,
    rs_send, rs4_p, rs1_z, rs4_z, rs1_p,
):
    me = lax.axis_index("tensor")
    core = lax.rem(me, 2)
    chip = me // 2
    z, xy = chip // NXY, lax.rem(chip, NXY)
    y, x = xy // NX, lax.rem(xy, NX)

    def plane(k):
        return lax.rem(y + k // NX, NY) * NX + lax.rem(x + lax.rem(k, NX), NX)

    def zed(k):
        return lax.rem(z + k, NZ)

    def dev(zz, pp):
        return {"tensor": (zz * NXY + pp) * 2 + core}

    sibling = {"tensor": chip * 2 + 1 - core}

    def send(src, dst, ssem, rsem, to):
        pltpu.make_async_remote_copy(src, dst, ssem, rsem, device_id=to, device_id_type=pl.DeviceIdType.MESH).start()

    def arrive(ref, sem):
        pltpu.make_async_copy(ref, ref, sem).wait()

    barrier = pltpu.get_barrier_semaphore()

    def greet(k, _):
        pl.semaphore_signal(barrier, inc=1, device_id=dev(zed(k), xy), device_id_type=pl.DeviceIdType.MESH)
        pl.semaphore_signal(barrier, inc=1, device_id=dev(z, plane(k)), device_id_type=pl.DeviceIdType.MESH)
        return 0

    lax.fori_loop(1, 8, greet, 0)
    pl.semaphore_signal(barrier, inc=1, device_id=sibling, device_id_type=pl.DeviceIdType.MESH)

    x_copy = pltpu.make_async_copy(x_ref, x_in, x_sem)
    x_copy.start()
    own = [(wg_ref, wg), (wu_ref, wu), (wd_ref, wd)]
    for i, (src, dst) in enumerate(own):
        pltpu.make_async_copy(src, dst.at[pl.ds(0, UNITS)], load_sem.at[i]).start()

    x_copy.wait()
    mine = x_in[...].astype(F32)
    for j in range(NJ):
        tmp[2 * j : 2 * j + 2, :] = mine[:, j * LANES : (j + 1) * LANES]
    rx[chip] = tmp[...].astype(BF16)

    pl.semaphore_wait(barrier, 15)

    low, high = pl.ds(0, CUT), pl.ds(CUT, ROWS - CUT)

    for k in NEAR[1:]:
        send(rx.at[chip, high], rx.at[chip, high], ag_send.at[0], ag4_z.at[k], dev(zed(k), xy))
    for k in FAR_PLANE:
        send(rx.at[chip, low], rx.at[chip, low], ag_send.at[1], ag1_p.at[k], dev(z, plane(k)))

    def spread4(i):
        block = zed(NEAR[i]) * NXY + xy
        if NEAR[i]:
            arrive(rx.at[block, high], ag4_z.at[NZ - NEAR[i]])
        for k in FAR_PLANE:
            send(rx.at[block, high], rx.at[block, high], ag_send.at[2], ag4_p.at[i], dev(z, plane(k)))

    def spread1(p):
        block = z * NXY + plane(p)
        if p:
            arrive(rx.at[block, low], ag1_p.at[(NX - p) % NX + p // NX * NX])
        for k in FAR[:-1]:
            send(rx.at[block, low], rx.at[block, low], ag_send.at[3], ag1_z.at[k], dev(zed(k), xy))

    spread4(0)
    spread1(0)
    for i, (src, dst) in enumerate(own):
        send(src, dst.at[pl.ds(UNITS, UNITS)], wsend.at[i], wrecv.at[i], sibling)
    for p in (4, 1, 3):
        spread1(p)
    for i in (1, 2):
        spread4(i)
    for p in (2, 5, 7):
        spread1(p)
    for i in (3, 4):
        spread4(i)
    spread1(6)
    for i in (5, 6, 7):
        spread4(i)

    def collect(zz, start, size, peak):
        for b in range(NXY):
            wide = rx[zz * NXY + b, start : start + size].astype(F32)
            fx[b * size : (b + 1) * size, :] = wide
            peak = jnp.maximum(peak, jnp.max(jnp.abs(wide).reshape(size // 8, 8, LANES), axis=0))
        for j in range(size // 2):
            pair = [fx[pl.ds(2 * j + t, 8, stride=size), :] for t in range(2)]
            at = start // 2 + j
            xs[pl.ds(pl.multiple_of(zz * 16, 16), 16), at * LANES : (at + 1) * LANES] = jnp.concatenate(pair, axis=0).astype(BF16)
        return peak

    def contract(w, start, size):
        cols = slice(start * LANES // 2, (start + size) * LANES // 2)
        return lax.dot_general(xs[:, cols], w[:, cols], (((1,), (1,)), ((), ())), preferred_element_type=F32)

    peak = jnp.zeros((8, LANES), F32)
    for i in range(NZ):
        if NEAR[i]:
            arrive(rx.at[pl.ds(0, NXY), low], ag1_z.at[NZ - NEAR[i]])
        peak = collect(zed(NEAR[i]), 0, CUT, peak)
    for i in range(NZ):
        arrive(rx.at[pl.ds(0, 7), high], ag4_p.at[i])
        peak = collect(zed(NEAR[i]), CUT, ROWS - CUT, peak)

    pk[0] = peak
    peak_copy = pltpu.make_async_remote_copy(
        pk.at[0], pk.at[1], pk_sem.at[0], pk_sem.at[1], device_id=sibling, device_id_type=pl.DeviceIdType.MESH
    )
    peak_copy.start()

    for i, (src, dst) in enumerate(own[:2]):
        pltpu.make_async_copy(src, dst.at[pl.ds(0, UNITS)], load_sem.at[i]).wait()
        arrive(dst.at[pl.ds(UNITS, UNITS)], wrecv.at[i])

    gate = contract(wg, 0, ROWS)
    up = contract(wu, 0, ROWS)

    peak_copy.wait()
    top = jnp.max(jnp.maximum(peak, pk[1]), keepdims=True)
    factor = TARGET / (top + EPSILON)
    gate = gate * factor
    hidden = (gate / (1.0 + jnp.exp(-gate)) * (up * factor)).astype(BF16)

    pltpu.make_async_copy(wd_ref, wd.at[pl.ds(0, UNITS)], load_sem.at[2]).wait()
    arrive(wd.at[pl.ds(UNITS, UNITS)], wrecv.at[2])
    part[...] = jnp.dot(hidden, wd[...], preferred_element_type=F32)

    for i in range(NZ):
        zz = zed(FAR[i])
        for j in range(NJ):
            for t in range(2):
                rows = part[pl.ds(pl.multiple_of(zz * 16 + t * 8, 8), 8), j * LANES : (j + 1) * LANES]
                sums[pl.ds(zz * (NXY * ROWS) + 2 * j + t, 8, stride=ROWS), :] = rows
        for b in range(NXY):
            sb[zz * NXY + b] = sums[pl.ds(pl.multiple_of((zz * NXY + b) * ROWS, ROWS), ROWS), :].astype(BF16)

        if FAR[i]:
            send(sb.at[pl.ds(zz * NXY, NXY), low], ra1.at[i], rs_send.at[1], rs1_z.at[i], dev(zz, xy))
        for k in FAR_PLANE:
            send(sb.at[zz * NXY + plane(k), high], ra4.at[i, k - 1], rs_send.at[0], rs4_p.at[i], dev(z, plane(k)))

    def mine_of(block, start, size):
        return sums[pl.ds(pl.multiple_of(block * ROWS + start, 16), size), :]

    def gather4(i):
        zz = zed(FAR[i])
        arrive(ra4.at[i], rs4_p.at[i])
        total = mine_of(zz * NXY + xy, CUT, ROWS - CUT)
        for k in range(7):
            total = total + ra4[i, k].astype(F32)
        if FAR[i]:
            sb4[i] = total.astype(BF16)
            send(sb4.at[i], rb4.at[i], rs_send.at[2], rs4_z.at[i], dev(zz, xy))
        else:
            tmp[CUT:, :] = total

    def gather1():
        for i in range(7):
            arrive(ra1.at[i], rs1_z.at[i])

        for k in FAR_PLANE:
            p = plane(k)
            total = mine_of(z * NXY + p, 0, CUT)
            for i in range(7):
                total = total + ra1[i, p].astype(F32)
            sb1[k] = total.astype(BF16)
            send(sb1.at[k], rb1.at[k], rs_send.at[3], rs1_p.at[k], dev(z, p))

        total = mine_of(chip, 0, CUT)
        for i in range(7):
            total = total + ra1[i, xy].astype(F32)
        tmp[:CUT, :] = total

    for i in range(NZ):
        gather4(i)
    gather1()

    for i in range(7):
        arrive(rb4.at[i], rs4_z.at[i])
        tmp[CUT:, :] += rb4[i].astype(F32)
    for k in range(1, 8):
        arrive(rb1.at[k], rs1_p.at[k])
        tmp[:CUT, :] += rb1[k].astype(F32)
    for j in range(NJ):
        o_ref[:, j * LANES : (j + 1) * LANES] = tmp[2 * j : 2 * j + 2, :].astype(BF16)

    for i, (src, dst) in enumerate(own):
        arrive(dst.at[pl.ds(UNITS, UNITS)], wsend.at[i])
    arrive(rx.at[pl.ds(0, 7), high], ag_send.at[0])
    arrive(rx.at[pl.ds(0, 7), low], ag_send.at[1])
    arrive(rx.at[pl.ds(0, 56), high], ag_send.at[2])
    arrive(rx.at[pl.ds(0, 56), low], ag_send.at[3])
    arrive(sb.at[pl.ds(0, 56), high], rs_send.at[0])
    arrive(sb.at[pl.ds(0, 56), low], rs_send.at[1])
    arrive(sb.at[pl.ds(0, 7), high], rs_send.at[2])
    arrive(sb.at[pl.ds(0, 7), low], rs_send.at[3])


def shards(tokens, gate_weight, up_weight, down_weight):
    vmem, hbm = pl.BlockSpec(memory_space=pltpu.VMEM), pl.BlockSpec(memory_space=pl.ANY)
    dma = pltpu.SemaphoreType.DMA
    high = ROWS - CUT
    return pl.pallas_call(
        kernel,
        out_shape=jax.ShapeDtypeStruct((2, D), BF16),
        in_specs=[hbm, hbm, hbm, hbm],
        out_specs=vmem,
        scratch_shapes=[
            pltpu.VMEM((2, D), BF16),
            pltpu.VMEM((CHIPS, ROWS, LANES), BF16),
            pltpu.VMEM((NXY * ROWS, LANES), F32),
            pltpu.VMEM((2 * CHIPS, D), BF16),
            pltpu.VMEM((2 * UNITS, D), BF16),
            pltpu.VMEM((2 * UNITS, D), BF16),
            pltpu.VMEM((2 * UNITS, D), BF16),
            pltpu.VMEM((2 * CHIPS, D), F32),
            pltpu.VMEM((CHIPS * ROWS, LANES), F32),
            pltpu.VMEM((CHIPS, ROWS, LANES), BF16),
            pltpu.VMEM((NZ, 7, high, LANES), BF16),
            pltpu.VMEM((7, NXY, CUT, LANES), BF16),
            pltpu.VMEM((7, high, LANES), BF16),
            pltpu.VMEM((8, CUT, LANES), BF16),
            pltpu.VMEM((7, high, LANES), BF16),
            pltpu.VMEM((8, CUT, LANES), BF16),
            pltpu.VMEM((ROWS, LANES), F32),
            pltpu.VMEM((2, 8, LANES), F32),
            dma, dma((3,)), dma((3,)), dma((3,)), dma((2,)),
            dma((4,)), dma((8,)), dma((8,)), dma((8,)), dma((8,)),
            dma((4,)), dma((8,)), dma((7,)), dma((7,)), dma((8,)),
        ],
        compiler_params=pltpu.CompilerParams(collective_id=0, has_side_effects=True, vmem_limit_bytes=60 << 20),
        name="ffn",
    )(tokens, gate_weight, up_weight, down_weight)


def solution(mesh):
    placed = (P(("dp", "tensor"), None), P("tensor", None), P("tensor", None), P("tensor", None))
    return jax.shard_map(
        shards, mesh=mesh, in_specs=placed, out_specs=P(("dp", "tensor"), None), check_vma=False
    )
```

```python
import jax
import jax.numpy as jnp
from jax import lax
from jax.experimental import pallas as pl
from jax.experimental.pallas import tpu as pltpu
from jax.sharding import PartitionSpec as P

TARGET = 16.0
EPSILON = 1e-06
F32, BF16 = jnp.float32, jnp.bfloat16

D = 4096
UNITS = 208
NZ, NX, NY = 8, 4, 2
NXY = NX * NY
CHIPS = NZ * NXY
LANES = 128
NJ = D // LANES
ROWS = 2 * NJ
CUT = 16
NEAR = (1, 7, 2, 6, 3, 5, 4)
FAR_PLANE = (6, 5, 7, 2, 4, 1, 3)
HALF = NZ // 2


def kernel(
    x_ref, wg_ref, wu_ref, wd_ref, o_ref,
    x_in, rx, fx, xs, wg, wu, wd, part, sums, sb, ra4, ra1, sb4, sb1, rb4, rb1, tmp, pk_mine, pk_z, pk_plane, pk_both,
    x_sem, load_sem, wsend, wrecv, pk_send, pk_zr, pk_pr, pk_sib,
    ag_send, ag4_z, ag1_p, ag4_p, ag1_z,
    rs_send, rs4_p, rs1_z, rs4_z, rs1_p,
):
    me = lax.axis_index("tensor")
    core = lax.rem(me, 2)
    chip = me // 2
    z, xy = chip // NXY, lax.rem(chip, NXY)
    y, x = xy // NX, lax.rem(xy, NX)

    def plane(k):
        return lax.rem(y + k // NX, NY) * NX + lax.rem(x + lax.rem(k, NX), NX)

    def zed(k):
        return lax.rem(z + k, NZ)

    def dev(zz, pp):
        return {"tensor": (zz * NXY + pp) * 2 + core}

    sibling = {"tensor": chip * 2 + 1 - core}

    def send(src, dst, ssem, rsem, to):
        pltpu.make_async_remote_copy(src, dst, ssem, rsem, device_id=to, device_id_type=pl.DeviceIdType.MESH).start()

    def arrive(ref, sem):
        pltpu.make_async_copy(ref, ref, sem).wait()

    barrier = pltpu.get_barrier_semaphore()

    def greet(k, _):
        pl.semaphore_signal(barrier, inc=1, device_id=dev(zed(k), xy), device_id_type=pl.DeviceIdType.MESH)
        pl.semaphore_signal(barrier, inc=1, device_id=dev(z, plane(k)), device_id_type=pl.DeviceIdType.MESH)
        return 0

    lax.fori_loop(1, 8, greet, 0)
    pl.semaphore_signal(barrier, inc=1, device_id=sibling, device_id_type=pl.DeviceIdType.MESH)

    x_copy = pltpu.make_async_copy(x_ref, x_in, x_sem)
    x_copy.start()
    own = [(wg_ref, wg), (wu_ref, wu), (wd_ref, wd)]
    for i, (src, dst) in enumerate(own):
        pltpu.make_async_copy(src, dst.at[pl.ds(0, UNITS)], load_sem.at[i]).start()

    x_copy.wait()
    mine = x_in[...].astype(F32)
    for j in range(NJ):
        tmp[2 * j : 2 * j + 2, :] = mine[:, j * LANES : (j + 1) * LANES]
    rx[chip] = tmp[...].astype(BF16)
    pk_mine[0] = jnp.max(jnp.abs(tmp[...]), axis=0, keepdims=True)

    pl.semaphore_wait(barrier, 15)

    low, high = pl.ds(0, CUT), pl.ds(CUT, ROWS - CUT)

    def arrive_if(here, ref, sem):
        pl.when(here)(lambda: arrive(ref, sem))

    for k in NEAR:
        send(pk_mine.at[0], pk_z.at[k], pk_send.at[0], pk_zr.at[k], dev(zed(k), xy))
    for k in NEAR:
        send(rx.at[chip, high], rx.at[chip, high], ag_send.at[0], ag4_z.at[k], dev(zed(k), xy))
    for k in FAR_PLANE:
        send(rx.at[chip, low], rx.at[chip, low], ag_send.at[1], ag1_p.at[k], dev(z, plane(k)))

    def to_plane(zz):
        block = zz * NXY + xy
        for k in FAR_PLANE:
            send(rx.at[block, high], rx.at[block, high], ag_send.at[2], ag4_p.at[zz], dev(z, plane(k)))

    def spread4(zz):
        @pl.when(zz != z)
        def _():
            arrive(rx.at[zz * NXY + xy, high], ag4_z.at[lax.rem(z - zz + NZ, NZ)])
            to_plane(zz)

    def spread1(p):
        block = z * NXY + plane(p)
        if p:
            arrive(rx.at[block, low], ag1_p.at[(NX - p) % NX + p // NX * NX])
        for k in NEAR[::-1]:
            send(rx.at[block, low], rx.at[block, low], ag_send.at[3], ag1_z.at[k], dev(zed(k), xy))

    upward = lax.rem(z + 2, NZ) < HALF
    early = z < HALF

    def nth(half, i):
        if half:
            return jnp.where(upward, NZ - 1 - i, HALF + i)
        return jnp.where(upward, i, HALF - 1 - i)

    to_plane(z)

    @pl.when(early)
    def _():
        for p in (0, 4, 1, 3):
            spread1(p)

    for i, (src, dst) in enumerate(own):
        send(src, dst.at[pl.ds(UNITS, UNITS)], wsend.at[i], wrecv.at[i], sibling)
    for i in (0, 1):
        spread4(nth(0, i))

    @pl.when(early)
    def _():
        for p in (2, 5, 7, 6):
            spread1(p)

    for i in (2, 3):
        spread4(nth(0, i))

    @pl.when(z >= HALF)
    def _():
        for p in (0, 4, 1, 3, 2, 5, 7, 6):
            spread1(p)

    for i in range(HALF):
        spread4(nth(1, i))

    peak = pk_mine[0]
    for k in NEAR:
        arrive(pk_z.at[k], pk_zr.at[k])
        peak = jnp.maximum(peak, pk_z[k])
    pk_mine[1] = peak
    for k in FAR_PLANE:
        send(pk_mine.at[1], pk_plane.at[k], pk_send.at[1], pk_pr.at[k], dev(z, plane(k)))

    def collect(zz):
        arrive_if(z != zz, rx.at[pl.ds(0, NXY), low], ag1_z.at[lax.rem(z - zz + NZ, NZ)])
        arrive(rx.at[pl.ds(0, 7), high], ag4_p.at[zz])
        for b in range(NXY):
            fx[b * ROWS : (b + 1) * ROWS, :] = rx[zz * NXY + b].astype(F32)
        for j in range(NJ):
            pair = [fx[pl.ds(2 * j + t, 8, stride=ROWS), :] for t in range(2)]
            xs[zz * 16 : (zz + 1) * 16, j * LANES : (j + 1) * LANES] = jnp.concatenate(pair, axis=0).astype(BF16)

    def contract(w, rows):
        return lax.dot_general(xs[rows], w[...], (((1,), (1,)), ((), ())), preferred_element_type=F32)

    def expand(gate, up, rows):
        gate = gate * factor
        hidden = (gate / (1.0 + jnp.exp(-gate)) * (up * factor)).astype(BF16)
        part[rows] = jnp.dot(hidden, wd[...], preferred_element_type=F32)

    def scatter(zz):
        for j in range(NJ):
            for t in range(2):
                rows = part[zz * 16 + t * 8 : zz * 16 + t * 8 + 8, j * LANES : (j + 1) * LANES]
                sums[pl.ds(zz * (NXY * ROWS) + 2 * j + t, 8, stride=ROWS), :] = rows
        for b in range(NXY):
            g = zz * NXY + b
            sb[g] = sums[g * ROWS : (g + 1) * ROWS, :].astype(BF16)

        @pl.when(z != zz)
        def _():
            k = lax.rem(zz - z + NZ, NZ)
            send(sb.at[pl.ds(zz * NXY, NXY), low], ra1.at[k], rs_send.at[1], rs1_z.at[k], dev(zz, xy))

        for k in FAR_PLANE:
            send(sb.at[zz * NXY + plane(k), high], ra4.at[zz, k - 1], rs_send.at[0], rs4_p.at[zz], dev(z, plane(k)))

    def mine_of(block, start, size):
        return sums[pl.ds(pl.multiple_of(block * ROWS + start, 16), size), :]

    def gather4(zz):
        arrive(ra4.at[zz], rs4_p.at[zz])
        total = mine_of(zz * NXY + xy, CUT, ROWS - CUT)
        for k in range(7):
            total = total + ra4[zz, k].astype(F32)

        @pl.when(z != zz)
        def _():
            k = lax.rem(zz - z + NZ, NZ)
            sb4[zz] = total.astype(BF16)
            send(sb4.at[zz], rb4.at[k], rs_send.at[2], rs4_z.at[k], dev(zz, xy))

        @pl.when(z == zz)
        def _():
            tmp[CUT:, :] = total

    def gather1():
        for k in NEAR:
            arrive(ra1.at[k], rs1_z.at[k])
        for k in (*FAR_PLANE, 0):
            p = plane(k)
            total = mine_of(z * NXY + p, 0, CUT)
            for i in NEAR:
                total = total + ra1[i, p].astype(F32)
            if k:
                sb1[k] = total.astype(BF16)
                send(sb1.at[k], rb1.at[k], rs_send.at[3], rs1_p.at[k], dev(z, p))
            else:
                tmp[:CUT, :] = total

    for zz in range(HALF):
        collect(zz)

    for k in FAR_PLANE:
        arrive(pk_plane.at[k], pk_pr.at[k])
        peak = jnp.maximum(peak, pk_plane[k])
    pk_mine[2] = peak
    send(pk_mine.at[2], pk_both.at[0], pk_send.at[2], pk_sib, sibling)
    for i, (src, dst) in enumerate(own[:2]):
        pltpu.make_async_copy(src, dst.at[pl.ds(0, UNITS)], load_sem.at[i]).wait()
        arrive(dst.at[pl.ds(UNITS, UNITS)], wrecv.at[i])
    first, second = slice(0, HALF * 16), slice(HALF * 16, NZ * 16)
    gate, up = contract(wg, first), contract(wu, first)

    arrive(pk_both.at[0], pk_sib)
    top = jnp.max(jnp.maximum(peak, pk_both[0]), keepdims=True)
    factor = TARGET / (top + EPSILON)
    pltpu.make_async_copy(wd_ref, wd.at[pl.ds(0, UNITS)], load_sem.at[2]).wait()
    arrive(wd.at[pl.ds(UNITS, UNITS)], wrecv.at[2])
    expand(gate, up, first)

    for zz in range(HALF):
        scatter(zz)

    for zz in range(HALF, NZ):
        collect(zz)

    gate, up = contract(wg, second), contract(wu, second)
    expand(gate, up, second)

    for zz in range(HALF, NZ):
        scatter(zz)

    for zz in range(HALF):
        gather4(zz)
    pl.when(early)(gather1)

    for zz in range(HALF, NZ):
        gather4(zz)
    pl.when(z >= HALF)(gather1)

    for k in NEAR:
        arrive(rb4.at[k], rs4_z.at[k])
        tmp[CUT:, :] += rb4[k].astype(F32)
    for k in FAR_PLANE:
        arrive(rb1.at[k], rs1_p.at[k])
        tmp[:CUT, :] += rb1[k].astype(F32)
    for j in range(NJ):
        o_ref[:, j * LANES : (j + 1) * LANES] = tmp[2 * j : 2 * j + 2, :].astype(BF16)

    for i, (src, dst) in enumerate(own):
        arrive(dst.at[pl.ds(UNITS, UNITS)], wsend.at[i])
    arrive(pk_z.at[pl.ds(0, 7)], pk_send.at[0])
    arrive(pk_plane.at[pl.ds(0, 7)], pk_send.at[1])
    arrive(pk_both.at[0], pk_send.at[2])
    arrive(rx.at[pl.ds(0, 7), high], ag_send.at[0])
    arrive(rx.at[pl.ds(0, 7), low], ag_send.at[1])
    arrive(rx.at[pl.ds(0, 56), high], ag_send.at[2])
    arrive(rx.at[pl.ds(0, 56), low], ag_send.at[3])
    arrive(sb.at[pl.ds(0, 56), high], rs_send.at[0])
    arrive(sb.at[pl.ds(0, 56), low], rs_send.at[1])
    arrive(sb.at[pl.ds(0, 7), high], rs_send.at[2])
    arrive(sb.at[pl.ds(0, 7), low], rs_send.at[3])


def shards(tokens, gate_weight, up_weight, down_weight):
    vmem, hbm = pl.BlockSpec(memory_space=pltpu.VMEM), pl.BlockSpec(memory_space=pl.ANY)
    dma = pltpu.SemaphoreType.DMA
    high = ROWS - CUT
    return pl.pallas_call(
        kernel,
        out_shape=jax.ShapeDtypeStruct((2, D), BF16),
        in_specs=[hbm, hbm, hbm, hbm],
        out_specs=vmem,
        scratch_shapes=[
            pltpu.VMEM((2, D), BF16),
            pltpu.VMEM((CHIPS, ROWS, LANES), BF16),
            pltpu.VMEM((NXY * ROWS, LANES), F32),
            pltpu.VMEM((2 * CHIPS, D), BF16),
            pltpu.VMEM((2 * UNITS, D), BF16),
            pltpu.VMEM((2 * UNITS, D), BF16),
            pltpu.VMEM((2 * UNITS, D), BF16),
            pltpu.VMEM((2 * CHIPS, D), F32),
            pltpu.VMEM((CHIPS * ROWS, LANES), F32),
            pltpu.VMEM((CHIPS, ROWS, LANES), BF16),
            pltpu.VMEM((NZ, 7, high, LANES), BF16),
            pltpu.VMEM((8, NXY, CUT, LANES), BF16),
            pltpu.VMEM((8, high, LANES), BF16),
            pltpu.VMEM((8, CUT, LANES), BF16),
            pltpu.VMEM((8, high, LANES), BF16),
            pltpu.VMEM((8, CUT, LANES), BF16),
            pltpu.VMEM((ROWS, LANES), F32),
            pltpu.VMEM((3, 1, LANES), F32),
            pltpu.VMEM((8, 1, LANES), F32),
            pltpu.VMEM((8, 1, LANES), F32),
            pltpu.VMEM((1, 1, LANES), F32),
            dma, dma((3,)), dma((3,)), dma((3,)), dma((3,)), dma((8,)), dma((8,)), dma,
            dma((4,)), dma((8,)), dma((8,)), dma((8,)), dma((8,)),
            dma((4,)), dma((8,)), dma((8,)), dma((8,)), dma((8,)),
        ],
        compiler_params=pltpu.CompilerParams(collective_id=0, has_side_effects=True, vmem_limit_bytes=60 << 20),
        name="ffn",
    )(tokens, gate_weight, up_weight, down_weight)


def solution(mesh):
    placed = (P(("dp", "tensor"), None), P("tensor", None), P("tensor", None), P("tensor", None))
    return jax.shard_map(
        shards, mesh=mesh, in_specs=placed, out_specs=P(("dp", "tensor"), None), check_vma=False
    )
```

```python
import jax
import jax.numpy as jnp
from jax import lax
from jax.experimental import pallas as pl
from jax.experimental.pallas import tpu as pltpu
from jax.sharding import PartitionSpec as P

TARGET = 16.0
EPSILON = 1e-06
F32, BF16 = jnp.float32, jnp.bfloat16

D = 4096
UNITS = 208
NZ, NX, NY = 8, 4, 2
NXY = NX * NY
CHIPS = NZ * NXY
LANES = 128
NJ = D // LANES
ROWS = 2 * NJ
CUT = 16
NEAR = (1, 7, 2, 6, 3, 5, 4)
FAR_PLANE = (6, 5, 7, 2, 4, 1, 3)
HALF = NZ // 2


def kernel(
    x_ref, wg_ref, wu_ref, wd_ref, o_ref,
    x_in, rx, fx, xs, wg, wu, wd, part, sums, sb, ra4, ra1, sb4, sb1, rb4, rb1, tmp, pk_mine, pk_z, pk_plane, pk_both,
    x_sem, load_sem, wsend, wrecv, pk_send, pk_zr, pk_pr, pk_sib,
    here_sib, ag_send, ag4_z, ag1_p, ag4_p, ag1_z,
    rs_send, rs4_p, rs1_z, rs4_z, rs1_p,
):
    me = lax.axis_index("tensor")
    core = lax.rem(me, 2)
    chip = me // 2
    z, xy = chip // NXY, lax.rem(chip, NXY)
    y, x = xy // NX, lax.rem(xy, NX)

    def plane(k):
        return lax.rem(y + k // NX, NY) * NX + lax.rem(x + lax.rem(k, NX), NX)

    def zed(k):
        return lax.rem(z + k, NZ)

    def dev(zz, pp):
        return {"tensor": (zz * NXY + pp) * 2 + core}

    sibling = {"tensor": chip * 2 + 1 - core}

    def send(src, dst, ssem, rsem, to):
        pltpu.make_async_remote_copy(src, dst, ssem, rsem, device_id=to, device_id_type=pl.DeviceIdType.MESH).start()

    def arrive(ref, sem):
        pltpu.make_async_copy(ref, ref, sem).wait()

    barrier = pltpu.get_barrier_semaphore()

    def greet(k, _):
        pl.semaphore_signal(barrier, inc=1, device_id=dev(zed(k), xy), device_id_type=pl.DeviceIdType.MESH)
        pl.semaphore_signal(barrier, inc=1, device_id=dev(z, plane(k)), device_id_type=pl.DeviceIdType.MESH)
        return 0

    lax.fori_loop(1, 8, greet, 0)
    @pl.when(core == 0)
    def _():
        pl.semaphore_signal(barrier, inc=1, device_id=sibling, device_id_type=pl.DeviceIdType.MESH)

    x_copy = pltpu.make_async_copy(x_ref, x_in, x_sem)
    x_copy.start()
    own = [(wg_ref, wg), (wu_ref, wu), (wd_ref, wd)]
    for i, (src, dst) in enumerate(own):
        pltpu.make_async_copy(src, dst.at[pl.ds(0, UNITS)], load_sem.at[i]).start()

    x_copy.wait()
    mine = x_in[...].astype(F32)
    for j in range(NJ):
        tmp[2 * j : 2 * j + 2, :] = mine[:, j * LANES : (j + 1) * LANES]
    rx[chip] = tmp[...].astype(BF16)
    pk_mine[0] = jnp.max(jnp.abs(tmp[...]), axis=0, keepdims=True)

    pl.semaphore_wait(barrier, 14 + core)

    @pl.when(core == 1)
    def _():
        pl.semaphore_signal(here_sib, inc=1, device_id=sibling, device_id_type=pl.DeviceIdType.MESH)

    low, high = pl.ds(0, CUT), pl.ds(CUT, ROWS - CUT)

    def arrive_if(here, ref, sem):
        pl.when(here)(lambda: arrive(ref, sem))

    for k in NEAR:
        send(pk_mine.at[0], pk_z.at[k], pk_send.at[0], pk_zr.at[k], dev(zed(k), xy))
    for k in NEAR:
        send(rx.at[chip, high], rx.at[chip, high], ag_send.at[0], ag4_z.at[k], dev(zed(k), xy))
    for k in FAR_PLANE:
        send(rx.at[chip, low], rx.at[chip, low], ag_send.at[1], ag1_p.at[k], dev(z, plane(k)))

    def to_plane(zz):
        block = zz * NXY + xy
        for k in FAR_PLANE:
            send(rx.at[block, high], rx.at[block, high], ag_send.at[2], ag4_p.at[zz], dev(z, plane(k)))

    def spread4(zz):
        arrive(rx.at[zz * NXY + xy, high], ag4_z.at[lax.rem(z - zz + NZ, NZ)])
        to_plane(zz)

    def spread1(p):
        block = z * NXY + plane(p)
        if p:
            arrive(rx.at[block, low], ag1_p.at[(NX - p) % NX + p // NX * NX])
        for k in NEAR[::-1]:
            send(rx.at[block, low], rx.at[block, low], ag_send.at[3], ag1_z.at[k], dev(zed(k), xy))

    early = z < HALF
    to_plane(z)
    def weights_to_sibling():
        for i, (src, dst) in enumerate(own):
            send(src, dst.at[pl.ds(UNITS, UNITS)], wsend.at[i], wrecv.at[i], sibling)

    pl.when(core == 1)(weights_to_sibling)
    for k in (1, 7):
        spread4(zed(k))

    @pl.when(core == 0)
    def _():
        pl.semaphore_wait(here_sib, 1)
        weights_to_sibling()

    for k in (2, 6):
        spread4(zed(k))
    for p in range(1, 8):
        arrive(rx.at[0, low], ag1_p.at[p])
    for k in NEAR[::-1]:
        blocks = rx.at[pl.ds(z * NXY, NXY), low]
        send(blocks, blocks, ag_send.at[3], ag1_z.at[k], dev(zed(k), xy))
    for k in (3, 5, 4):
        spread4(zed(k))

    peak = pk_mine[0]
    for k in NEAR:
        arrive(pk_z.at[k], pk_zr.at[k])
        peak = jnp.maximum(peak, pk_z[k])
    pk_mine[1] = peak
    for k in FAR_PLANE:
        send(pk_mine.at[1], pk_plane.at[k], pk_send.at[1], pk_pr.at[k], dev(z, plane(k)))

    def collect(zz, start, size):
        for b in range(NXY):
            fx[b * size : (b + 1) * size, :] = rx[zz * NXY + b, start : start + size].astype(F32)
        for j in range(size // 2):
            pair = [fx[pl.ds(2 * j + t, 8, stride=size), :] for t in range(2)]
            at = start // 2 + j
            xs[zz * 16 : (zz + 1) * 16, at * LANES : (at + 1) * LANES] = jnp.concatenate(pair, axis=0).astype(BF16)

    def contract(w, start, size):
        cols = slice(start * LANES // 2, (start + size) * LANES // 2)
        return lax.dot_general(xs[:, cols], w[:, cols], (((1,), (1,)), ((), ())), preferred_element_type=F32)

    def expand(gate, up):
        gate = gate * factor
        hidden = (gate / (1.0 + jnp.exp(-gate)) * (up * factor)).astype(BF16)
        part[...] = jnp.dot(hidden, wd[...], preferred_element_type=F32)

    def lay_out(zz, start, size):
        for j in range(start // 2, (start + size) // 2):
            for t in range(2):
                rows = part[zz * 16 + t * 8 : zz * 16 + t * 8 + 8, j * LANES : (j + 1) * LANES]
                sums[pl.ds(zz * (NXY * ROWS) + 2 * j + t, 8, stride=ROWS), :] = rows
        for b in range(NXY):
            g = zz * NXY + b
            sb[g, start : start + size] = sums[g * ROWS + start : g * ROWS + start + size, :].astype(BF16)

    def scatter1():
        for zz in range(NZ):
            lay_out(zz, 0, CUT)
        for k in NEAR[::-1]:
            send(sb.at[pl.ds(zed(k) * NXY, NXY), low], ra1.at[k], rs_send.at[1], rs1_z.at[k], dev(zed(k), xy))

    def scatter4(zz):
        lay_out(zz, CUT, ROWS - CUT)
        for k in FAR_PLANE:
            send(sb.at[zz * NXY + plane(k), high], ra4.at[zz, k - 1], rs_send.at[0], rs4_p.at[zz], dev(z, plane(k)))

    def mine_of(block, start, size):
        return sums[pl.ds(pl.multiple_of(block * ROWS + start, 16), size), :]

    def gather4(zz):
        arrive(ra4.at[zz], rs4_p.at[zz])
        total = mine_of(zz * NXY + xy, CUT, ROWS - CUT)
        for k in range(7):
            total = total + ra4[zz, k].astype(F32)

        @pl.when(z != zz)
        def _():
            k = lax.rem(zz - z + NZ, NZ)
            sb4[zz] = total.astype(BF16)
            send(sb4.at[zz], rb4.at[k], rs_send.at[2], rs4_z.at[k], dev(zz, xy))

        @pl.when(z == zz)
        def _():
            tmp[CUT:, :] = total

    def gather1():
        for k in NEAR:
            arrive(ra1.at[k], rs1_z.at[k])
        for k in (*FAR_PLANE, 0):
            p = plane(k)
            total = mine_of(z * NXY + p, 0, CUT)
            for i in NEAR:
                total = total + ra1[i, p].astype(F32)
            if k:
                sb1[k] = total.astype(BF16)
                send(sb1.at[k], rb1.at[k], rs_send.at[3], rs1_p.at[k], dev(z, p))
            else:
                tmp[:CUT, :] = total

    for zz in range(NZ):
        arrive_if(z != zz, rx.at[pl.ds(0, NXY), low], ag1_z.at[lax.rem(z - zz + NZ, NZ)])
        collect(zz, 0, CUT)
    for k in FAR_PLANE:
        arrive(pk_plane.at[k], pk_pr.at[k])
        peak = jnp.maximum(peak, pk_plane[k])
    pk_mine[2] = peak
    send(pk_mine.at[2], pk_both.at[0], pk_send.at[2], pk_sib, sibling)
    for zz in range(NZ):
        arrive(rx.at[pl.ds(0, 7), high], ag4_p.at[zz])
        collect(zz, CUT, ROWS - CUT)

    for i, (src, dst) in enumerate(own[:2]):
        pltpu.make_async_copy(src, dst.at[pl.ds(0, UNITS)], load_sem.at[i]).wait()
        arrive(dst.at[pl.ds(UNITS, UNITS)], wrecv.at[i])
    gate = contract(wg, 0, ROWS)
    up = contract(wu, 0, ROWS)
    pltpu.make_async_copy(wd_ref, wd.at[pl.ds(0, UNITS)], load_sem.at[2]).wait()
    arrive(wd.at[pl.ds(UNITS, UNITS)], wrecv.at[2])
    arrive(pk_both.at[0], pk_sib)
    top = jnp.max(jnp.maximum(peak, pk_both[0]), keepdims=True)
    factor = TARGET / (top + EPSILON)
    expand(gate, up)

    scatter1()
    for zz in range(NZ):
        scatter4(zz)

    for zz in range(HALF):
        gather4(zz)
    pl.when(early)(gather1)
    for zz in range(HALF, NZ):
        gather4(zz)
    pl.when(z >= HALF)(gather1)

    for k in NEAR:
        arrive(rb4.at[k], rs4_z.at[k])
        tmp[CUT:, :] += rb4[k].astype(F32)
    for k in FAR_PLANE:
        arrive(rb1.at[k], rs1_p.at[k])
        tmp[:CUT, :] += rb1[k].astype(F32)
    for j in range(NJ):
        o_ref[:, j * LANES : (j + 1) * LANES] = tmp[2 * j : 2 * j + 2, :].astype(BF16)

    for i, (src, dst) in enumerate(own):
        arrive(dst.at[pl.ds(UNITS, UNITS)], wsend.at[i])
    arrive(pk_z.at[pl.ds(0, 7)], pk_send.at[0])
    arrive(pk_plane.at[pl.ds(0, 7)], pk_send.at[1])
    arrive(pk_both.at[0], pk_send.at[2])
    arrive(rx.at[pl.ds(0, 7), high], ag_send.at[0])
    arrive(rx.at[pl.ds(0, 7), low], ag_send.at[1])
    arrive(rx.at[pl.ds(0, 56), high], ag_send.at[2])
    arrive(rx.at[pl.ds(0, 56), low], ag_send.at[3])
    arrive(sb.at[pl.ds(0, 56), high], rs_send.at[0])
    arrive(sb.at[pl.ds(0, 56), low], rs_send.at[1])
    arrive(sb.at[pl.ds(0, 7), high], rs_send.at[2])
    arrive(sb.at[pl.ds(0, 7), low], rs_send.at[3])


def shards(tokens, gate_weight, up_weight, down_weight):
    vmem, hbm = pl.BlockSpec(memory_space=pltpu.VMEM), pl.BlockSpec(memory_space=pl.ANY)
    dma = pltpu.SemaphoreType.DMA
    high = ROWS - CUT
    return pl.pallas_call(
        kernel,
        out_shape=jax.ShapeDtypeStruct((2, D), BF16),
        in_specs=[hbm, hbm, hbm, hbm],
        out_specs=vmem,
        scratch_shapes=[
            pltpu.VMEM((2, D), BF16),
            pltpu.VMEM((CHIPS, ROWS, LANES), BF16),
            pltpu.VMEM((NXY * ROWS, LANES), F32),
            pltpu.VMEM((2 * CHIPS, D), BF16),
            pltpu.VMEM((2 * UNITS, D), BF16),
            pltpu.VMEM((2 * UNITS, D), BF16),
            pltpu.VMEM((2 * UNITS, D), BF16),
            pltpu.VMEM((2 * CHIPS, D), F32),
            pltpu.VMEM((CHIPS * ROWS, LANES), F32),
            pltpu.VMEM((CHIPS, ROWS, LANES), BF16),
            pltpu.VMEM((NZ, 7, high, LANES), BF16),
            pltpu.VMEM((8, NXY, CUT, LANES), BF16),
            pltpu.VMEM((8, high, LANES), BF16),
            pltpu.VMEM((8, CUT, LANES), BF16),
            pltpu.VMEM((8, high, LANES), BF16),
            pltpu.VMEM((8, CUT, LANES), BF16),
            pltpu.VMEM((ROWS, LANES), F32),
            pltpu.VMEM((3, 1, LANES), F32),
            pltpu.VMEM((8, 1, LANES), F32),
            pltpu.VMEM((8, 1, LANES), F32),
            pltpu.VMEM((1, 1, LANES), F32),
            dma, dma((3,)), dma((3,)), dma((3,)), dma((3,)), dma((8,)), dma((8,)), dma,
            pltpu.SemaphoreType.REGULAR,
            dma((4,)), dma((8,)), dma((8,)), dma((8,)), dma((8,)),
            dma((4,)), dma((8,)), dma((8,)), dma((8,)), dma((8,)),
        ],
        compiler_params=pltpu.CompilerParams(collective_id=0, has_side_effects=True, vmem_limit_bytes=60 << 20),
        name="ffn",
    )(tokens, gate_weight, up_weight, down_weight)


def solution(mesh):
    placed = (P(("dp", "tensor"), None), P("tensor", None), P("tensor", None), P("tensor", None))
    return jax.shard_map(
        shards, mesh=mesh, in_specs=placed, out_specs=P(("dp", "tensor"), None), check_vma=False
    )
```

```python
import jax
import jax.numpy as jnp
from jax import lax
from jax.experimental import pallas as pl
from jax.experimental.pallas import tpu as pltpu
from jax.sharding import PartitionSpec as P

TARGET = 16.0
EPSILON = 1e-06
F32, BF16 = jnp.float32, jnp.bfloat16

D = 4096
UNITS = 208
NZ, NX, NY = 8, 4, 2
NXY = NX * NY
CHIPS = NZ * NXY
LANES = 128
NJ = D // LANES
ROWS = 2 * NJ
PITCH = ROWS + 8
CUT = 16
NEAR = (1, 7, 2, 6, 3, 5, 4)
FAR_PLANE = (6, 5, 7, 2, 4, 1, 3)
HALF = NZ // 2


def kernel(
    x_ref, wg_ref, wu_ref, wd_ref, o_ref,
    x_in, rx, fx, xs, wg, wu, wd, part, sums, sb, ra4, ra1, sb4, sb1, rb4, rb1, tmp, pk_mine, pk_z, pk_plane, pk_both,
    x_sem, load_sem, wsend, wrecv, pk_send, pk_zr, pk_pr, pk_sib,
    here_sib, ag_send, ag4_z, ag1_p, ag4_p, ag1_z,
    rs_send, rs4_p, rs1_z, rs4_z, rs1_p,
):
    me = lax.axis_index("tensor")
    core = lax.rem(me, 2)
    chip = me // 2
    z, xy = chip // NXY, lax.rem(chip, NXY)
    y, x = xy // NX, lax.rem(xy, NX)

    def plane(k):
        return lax.rem(y + k // NX, NY) * NX + lax.rem(x + lax.rem(k, NX), NX)

    def zed(k):
        return lax.rem(z + k, NZ)

    def dev(zz, pp):
        return {"tensor": (zz * NXY + pp) * 2 + core}

    sibling = {"tensor": chip * 2 + 1 - core}

    def send(src, dst, ssem, rsem, to):
        pltpu.make_async_remote_copy(src, dst, ssem, rsem, device_id=to, device_id_type=pl.DeviceIdType.MESH).start()

    def arrive(ref, sem):
        pltpu.make_async_copy(ref, ref, sem).wait()

    barrier = pltpu.get_barrier_semaphore()

    def greet(k, _):
        pl.semaphore_signal(barrier, inc=1, device_id=dev(zed(k), xy), device_id_type=pl.DeviceIdType.MESH)
        pl.semaphore_signal(barrier, inc=1, device_id=dev(z, plane(k)), device_id_type=pl.DeviceIdType.MESH)
        return 0

    lax.fori_loop(1, 8, greet, 0)
    @pl.when(core == 0)
    def _():
        pl.semaphore_signal(barrier, inc=1, device_id=sibling, device_id_type=pl.DeviceIdType.MESH)

    x_copy = pltpu.make_async_copy(x_ref, x_in, x_sem)
    x_copy.start()
    own = [(wg_ref, wg), (wu_ref, wu), (wd_ref, wd)]
    for i, (src, dst) in enumerate(own):
        pltpu.make_async_copy(src, dst.at[pl.ds(0, UNITS)], load_sem.at[i]).start()

    x_copy.wait()
    mine = x_in[...].astype(F32)
    for j in range(NJ):
        tmp[2 * j : 2 * j + 2, :] = mine[:, j * LANES : (j + 1) * LANES]
    rx[chip] = tmp[...].astype(BF16)
    pk_mine[0] = jnp.max(jnp.abs(tmp[...]), axis=0, keepdims=True)

    pl.semaphore_wait(barrier, 14 + core)

    @pl.when(core == 1)
    def _():
        pl.semaphore_signal(here_sib, inc=1, device_id=sibling, device_id_type=pl.DeviceIdType.MESH)

    low, high = pl.ds(0, CUT), pl.ds(CUT, ROWS - CUT)

    def arrive_if(here, ref, sem):
        pl.when(here)(lambda: arrive(ref, sem))

    for k in NEAR:
        send(pk_mine.at[0], pk_z.at[k], pk_send.at[0], pk_zr.at[k], dev(zed(k), xy))
    for k in NEAR:
        send(rx.at[chip, high], rx.at[chip, high], ag_send.at[0], ag4_z.at[k], dev(zed(k), xy))
    for k in FAR_PLANE:
        send(rx.at[chip, low], rx.at[chip, low], ag_send.at[1], ag1_p.at[k], dev(z, plane(k)))

    def to_plane(zz):
        block = zz * NXY + xy
        for k in FAR_PLANE:
            send(rx.at[block, high], rx.at[block, high], ag_send.at[2], ag4_p.at[zz], dev(z, plane(k)))

    def spread4(zz):
        arrive(rx.at[zz * NXY + xy, high], ag4_z.at[lax.rem(z - zz + NZ, NZ)])
        to_plane(zz)

    def spread1(p):
        block = z * NXY + plane(p)
        if p:
            arrive(rx.at[block, low], ag1_p.at[(NX - p) % NX + p // NX * NX])
        for k in NEAR[::-1]:
            send(rx.at[block, low], rx.at[block, low], ag_send.at[3], ag1_z.at[k], dev(zed(k), xy))

    early = z < HALF
    to_plane(z)
    def weights_to_sibling():
        for i, (src, dst) in enumerate(own):
            send(src, dst.at[pl.ds(UNITS, UNITS)], wsend.at[i], wrecv.at[i], sibling)

    pl.when(core == 1)(weights_to_sibling)
    for k in (1, 7):
        spread4(zed(k))

    @pl.when(core == 0)
    def _():
        pl.semaphore_wait(here_sib, 1)
        weights_to_sibling()

    for k in (2, 6):
        spread4(zed(k))
    for p in range(1, 8):
        arrive(rx.at[0, low], ag1_p.at[p])
    for k in NEAR[::-1]:
        blocks = rx.at[pl.ds(z * NXY, NXY), low]
        send(blocks, blocks, ag_send.at[3], ag1_z.at[k], dev(zed(k), xy))
    for k in (3, 5, 4):
        spread4(zed(k))

    peak = pk_mine[0]
    for k in NEAR:
        arrive(pk_z.at[k], pk_zr.at[k])
        peak = jnp.maximum(peak, pk_z[k])
    pk_mine[1] = peak
    for k in FAR_PLANE:
        send(pk_mine.at[1], pk_plane.at[k], pk_send.at[1], pk_pr.at[k], dev(z, plane(k)))

    def collect(zz, start, size):
        for b in range(NXY):
            fx[b * size : (b + 1) * size, :] = rx[zz * NXY + b, start : start + size].astype(F32)
        for j in range(size // 2):
            pair = [fx[pl.ds(2 * j + t, 8, stride=size), :] for t in range(2)]
            at = start // 2 + j
            xs[zz * 16 : (zz + 1) * 16, at * LANES : (at + 1) * LANES] = jnp.concatenate(pair, axis=0).astype(BF16)

    def contract(w, start, size):
        cols = slice(start * LANES // 2, (start + size) * LANES // 2)
        return lax.dot_general(xs[:, cols], w[:, cols], (((1,), (1,)), ((), ())), preferred_element_type=F32)

    def expand(gate, up):
        gate = gate * factor
        hidden = (gate / (1.0 + jnp.exp(-gate)) * (up * factor)).astype(BF16)
        part[...] = jnp.dot(hidden, wd[...], preferred_element_type=F32)

    def lay_out(zz, start, size):
        for j in range(start // 2, (start + size) // 2):
            for t in range(2):
                rows = part[zz * 16 + t * 8 : zz * 16 + t * 8 + 8, j * LANES : (j + 1) * LANES]
                sums[pl.ds(zz * (NXY * PITCH) + 2 * j + t, 8, stride=PITCH), :] = rows
        for b in range(NXY):
            g = zz * NXY + b
            sb[g, start : start + size] = sums[g * PITCH + start : g * PITCH + start + size, :].astype(BF16)

    def scatter1():
        for zz in range(NZ):
            lay_out(zz, 0, CUT)
        for k in NEAR[::-1]:
            send(sb.at[pl.ds(zed(k) * NXY, NXY), low], ra1.at[k], rs_send.at[1], rs1_z.at[k], dev(zed(k), xy))

    def scatter4(zz):
        lay_out(zz, CUT, ROWS - CUT)
        for k in FAR_PLANE:
            send(sb.at[zz * NXY + plane(k), high], ra4.at[zz, k - 1], rs_send.at[0], rs4_p.at[zz], dev(z, plane(k)))

    def mine_of(block, start, size):
        return sums[pl.ds(pl.multiple_of(block * PITCH + start, 8), size), :]

    def gather4(zz):
        arrive(ra4.at[zz], rs4_p.at[zz])
        total = mine_of(zz * NXY + xy, CUT, ROWS - CUT)
        for k in range(7):
            total = total + ra4[zz, k].astype(F32)

        @pl.when(z != zz)
        def _():
            k = lax.rem(zz - z + NZ, NZ)
            sb4[zz] = total.astype(BF16)
            send(sb4.at[zz], rb4.at[k], rs_send.at[2], rs4_z.at[k], dev(zz, xy))

        @pl.when(z == zz)
        def _():
            tmp[CUT:, :] = total

    def gather1():
        for k in NEAR:
            arrive(ra1.at[k], rs1_z.at[k])
        for k in (*FAR_PLANE, 0):
            p = plane(k)
            total = mine_of(z * NXY + p, 0, CUT)
            for i in NEAR:
                total = total + ra1[i, p].astype(F32)
            if k:
                sb1[k] = total.astype(BF16)
                send(sb1.at[k], rb1.at[k], rs_send.at[3], rs1_p.at[k], dev(z, p))
            else:
                tmp[:CUT, :] = total

    for zz in range(NZ):
        arrive_if(z != zz, rx.at[pl.ds(0, NXY), low], ag1_z.at[lax.rem(z - zz + NZ, NZ)])
        collect(zz, 0, CUT)
    for k in FAR_PLANE:
        arrive(pk_plane.at[k], pk_pr.at[k])
        peak = jnp.maximum(peak, pk_plane[k])
    pk_mine[2] = peak
    send(pk_mine.at[2], pk_both.at[0], pk_send.at[2], pk_sib, sibling)
    for zz in range(NZ):
        arrive(rx.at[pl.ds(0, 7), high], ag4_p.at[zz])
        collect(zz, CUT, ROWS - CUT)

    for i, (src, dst) in enumerate(own[:2]):
        pltpu.make_async_copy(src, dst.at[pl.ds(0, UNITS)], load_sem.at[i]).wait()
        arrive(dst.at[pl.ds(UNITS, UNITS)], wrecv.at[i])
    gate = contract(wg, 0, ROWS)
    up = contract(wu, 0, ROWS)
    pltpu.make_async_copy(wd_ref, wd.at[pl.ds(0, UNITS)], load_sem.at[2]).wait()
    arrive(wd.at[pl.ds(UNITS, UNITS)], wrecv.at[2])
    arrive(pk_both.at[0], pk_sib)
    top = jnp.max(jnp.maximum(peak, pk_both[0]), keepdims=True)
    factor = TARGET / (top + EPSILON)
    expand(gate, up)

    scatter1()
    for zz in range(NZ):
        scatter4(zz)

    for zz in range(HALF):
        gather4(zz)
    pl.when(early)(gather1)
    for zz in range(HALF, NZ):
        gather4(zz)
    pl.when(z >= HALF)(gather1)

    for k in NEAR:
        arrive(rb4.at[k], rs4_z.at[k])
        tmp[CUT:, :] += rb4[k].astype(F32)
    for k in FAR_PLANE:
        arrive(rb1.at[k], rs1_p.at[k])
        tmp[:CUT, :] += rb1[k].astype(F32)
    for j in range(NJ):
        o_ref[:, j * LANES : (j + 1) * LANES] = tmp[2 * j : 2 * j + 2, :].astype(BF16)

    for i, (src, dst) in enumerate(own):
        arrive(dst.at[pl.ds(UNITS, UNITS)], wsend.at[i])
    arrive(pk_z.at[pl.ds(0, 7)], pk_send.at[0])
    arrive(pk_plane.at[pl.ds(0, 7)], pk_send.at[1])
    arrive(pk_both.at[0], pk_send.at[2])
    arrive(rx.at[pl.ds(0, 7), high], ag_send.at[0])
    arrive(rx.at[pl.ds(0, 7), low], ag_send.at[1])
    arrive(rx.at[pl.ds(0, 56), high], ag_send.at[2])
    arrive(rx.at[pl.ds(0, 56), low], ag_send.at[3])
    arrive(sb.at[pl.ds(0, 56), high], rs_send.at[0])
    arrive(sb.at[pl.ds(0, 56), low], rs_send.at[1])
    arrive(sb.at[pl.ds(0, 7), high], rs_send.at[2])
    arrive(sb.at[pl.ds(0, 7), low], rs_send.at[3])


def shards(tokens, gate_weight, up_weight, down_weight):
    vmem, hbm = pl.BlockSpec(memory_space=pltpu.VMEM), pl.BlockSpec(memory_space=pl.ANY)
    dma = pltpu.SemaphoreType.DMA
    high = ROWS - CUT
    return pl.pallas_call(
        kernel,
        out_shape=jax.ShapeDtypeStruct((2, D), BF16),
        in_specs=[hbm, hbm, hbm, hbm],
        out_specs=vmem,
        scratch_shapes=[
            pltpu.VMEM((2, D), BF16),
            pltpu.VMEM((CHIPS, ROWS, LANES), BF16),
            pltpu.VMEM((NXY * ROWS, LANES), F32),
            pltpu.VMEM((2 * CHIPS, D), BF16),
            pltpu.VMEM((2 * UNITS, D), BF16),
            pltpu.VMEM((2 * UNITS, D), BF16),
            pltpu.VMEM((2 * UNITS, D), BF16),
            pltpu.VMEM((2 * CHIPS, D), F32),
            pltpu.VMEM((CHIPS * PITCH, LANES), F32),
            pltpu.VMEM((CHIPS, ROWS, LANES), BF16),
            pltpu.VMEM((NZ, 7, high, LANES), BF16),
            pltpu.VMEM((8, NXY, CUT, LANES), BF16),
            pltpu.VMEM((8, high, LANES), BF16),
            pltpu.VMEM((8, CUT, LANES), BF16),
            pltpu.VMEM((8, high, LANES), BF16),
            pltpu.VMEM((8, CUT, LANES), BF16),
            pltpu.VMEM((ROWS, LANES), F32),
            pltpu.VMEM((3, 1, LANES), F32),
            pltpu.VMEM((8, 1, LANES), F32),
            pltpu.VMEM((8, 1, LANES), F32),
            pltpu.VMEM((1, 1, LANES), F32),
            dma, dma((3,)), dma((3,)), dma((3,)), dma((3,)), dma((8,)), dma((8,)), dma,
            pltpu.SemaphoreType.REGULAR,
            dma((4,)), dma((8,)), dma((8,)), dma((8,)), dma((8,)),
            dma((4,)), dma((8,)), dma((8,)), dma((8,)), dma((8,)),
        ],
        compiler_params=pltpu.CompilerParams(collective_id=0, has_side_effects=True, vmem_limit_bytes=60 << 20),
        name="ffn",
    )(tokens, gate_weight, up_weight, down_weight)


def solution(mesh):
    placed = (P(("dp", "tensor"), None), P("tensor", None), P("tensor", None), P("tensor", None))
    return jax.shard_map(
        shards, mesh=mesh, in_specs=placed, out_specs=P(("dp", "tensor"), None), check_vma=False
    )
```

```python
import jax
import jax.numpy as jnp
from jax import lax
from jax.experimental import pallas as pl
from jax.experimental.pallas import tpu as pltpu
from jax.sharding import PartitionSpec as P

TARGET = 16.0
EPSILON = 1e-06
F32, BF16 = jnp.float32, jnp.bfloat16

D = 4096
UNITS = 208
NZ, NX, NY = 8, 4, 2
NXY = NX * NY
CHIPS = NZ * NXY
LANES = 128
NJ = D // LANES
ROWS = 2 * NJ
PITCH = ROWS + 8
CUT = 16
NEAR = (1, 7, 2, 6, 3, 5, 4)
FAR_PLANE = (6, 5, 7, 2, 4, 1, 3)
HALF = NZ // 2


def kernel(
    x_ref, wg_ref, wu_ref, wd_ref, o_ref,
    x_in, rx, fx, xs, wg, wu, wd, part, sums, sb, ra4, ra1, sb4, sb1, rb4, rb1, tmp, pk_mine, pk_z, pk_plane, pk_both,
    x_sem, load_sem, wsend, wrecv, pk_send, pk_zr, pk_pr, pk_sib,
    here_sib, ag_send, ag4_z, ag1_p, ag4_p, ag1_z,
    rs_send, rs4_p, rs1_z, rs4_z, rs1_p,
):
    me = lax.axis_index("tensor")
    core = lax.rem(me, 2)
    chip = me // 2
    z, xy = chip // NXY, lax.rem(chip, NXY)
    y, x = xy // NX, lax.rem(xy, NX)

    def plane(k):
        return lax.rem(y + k // NX, NY) * NX + lax.rem(x + lax.rem(k, NX), NX)

    def zed(k):
        return lax.rem(z + k, NZ)

    def dev(zz, pp):
        return {"tensor": (zz * NXY + pp) * 2 + core}

    sibling = {"tensor": chip * 2 + 1 - core}

    def send(src, dst, ssem, rsem, to):
        pltpu.make_async_remote_copy(src, dst, ssem, rsem, device_id=to, device_id_type=pl.DeviceIdType.MESH).start()

    def arrive(ref, sem):
        pltpu.make_async_copy(ref, ref, sem).wait()

    barrier = pltpu.get_barrier_semaphore()

    for k in NEAR[::-1]:
        pl.semaphore_signal(barrier, inc=1, device_id=dev(zed(k), xy), device_id_type=pl.DeviceIdType.MESH)
    for k in FAR_PLANE:
        pl.semaphore_signal(barrier, inc=1, device_id=dev(z, plane(k)), device_id_type=pl.DeviceIdType.MESH)
    @pl.when(core == 0)
    def _():
        pl.semaphore_signal(barrier, inc=1, device_id=sibling, device_id_type=pl.DeviceIdType.MESH)

    x_copy = pltpu.make_async_copy(x_ref, x_in, x_sem)
    x_copy.start()
    own = [(wg_ref, wg), (wu_ref, wu), (wd_ref, wd)]
    for i, (src, dst) in enumerate(own):
        pltpu.make_async_copy(src, dst.at[pl.ds(0, UNITS)], load_sem.at[i]).start()

    x_copy.wait()
    mine = x_in[...].astype(F32)
    for j in range(NJ):
        tmp[2 * j : 2 * j + 2, :] = mine[:, j * LANES : (j + 1) * LANES]
    rx[chip] = tmp[...].astype(BF16)
    pk_mine[0] = jnp.max(jnp.abs(tmp[...]), axis=0, keepdims=True)

    pl.semaphore_wait(barrier, 14 + core)

    @pl.when(core == 1)
    def _():
        pl.semaphore_signal(here_sib, inc=1, device_id=sibling, device_id_type=pl.DeviceIdType.MESH)

    low, high = pl.ds(0, CUT), pl.ds(CUT, ROWS - CUT)

    def each(start, stop, body):
        def step(i, _):
            body(i)
            return 0

        lax.fori_loop(start, stop, step, 0)

    def arrive_if(here, ref, sem):
        pl.when(here)(lambda: arrive(ref, sem))

    for k in NEAR:
        send(pk_mine.at[0], pk_z.at[k], pk_send.at[0], pk_zr.at[k], dev(zed(k), xy))
    for k in NEAR:
        send(rx.at[chip, high], rx.at[chip, high], ag_send.at[0], ag4_z.at[k], dev(zed(k), xy))
    for k in FAR_PLANE:
        send(rx.at[chip, low], rx.at[chip, low], ag_send.at[1], ag1_p.at[k], dev(z, plane(k)))

    def to_plane(zz):
        block = zz * NXY + xy
        for k in FAR_PLANE:
            send(rx.at[block, high], rx.at[block, high], ag_send.at[2], ag4_p.at[zz], dev(z, plane(k)))

    def spread4(zz):
        arrive(rx.at[zz * NXY + xy, high], ag4_z.at[lax.rem(z - zz + NZ, NZ)])
        to_plane(zz)

    def spread1(p):
        block = z * NXY + plane(p)
        if p:
            arrive(rx.at[block, low], ag1_p.at[(NX - p) % NX + p // NX * NX])
        for k in NEAR[::-1]:
            send(rx.at[block, low], rx.at[block, low], ag_send.at[3], ag1_z.at[k], dev(zed(k), xy))

    early = z < HALF
    to_plane(z)
    def weights_to_sibling():
        for i, (src, dst) in enumerate(own):
            send(src, dst.at[pl.ds(UNITS, UNITS)], wsend.at[i], wrecv.at[i], sibling)

    pl.when(core == 1)(weights_to_sibling)
    for k in (1, 7):
        spread4(zed(k))

    @pl.when(core == 0)
    def _():
        pl.semaphore_wait(here_sib, 1)
        weights_to_sibling()

    for k in (2, 6):
        spread4(zed(k))
    for p in range(1, 8):
        arrive(rx.at[0, low], ag1_p.at[p])
    for k in NEAR[::-1]:
        blocks = rx.at[pl.ds(z * NXY, NXY), low]
        send(blocks, blocks, ag_send.at[3], ag1_z.at[k], dev(zed(k), xy))
    for k in (3, 5, 4):
        spread4(zed(k))

    peak = pk_mine[0]
    for k in NEAR:
        arrive(pk_z.at[k], pk_zr.at[k])
        peak = jnp.maximum(peak, pk_z[k])
    pk_mine[1] = peak
    for k in FAR_PLANE:
        send(pk_mine.at[1], pk_plane.at[k], pk_send.at[1], pk_pr.at[k], dev(z, plane(k)))

    def collect(zz, start, size):
        for b in range(NXY):
            fx[b * size : (b + 1) * size, :] = rx[zz * NXY + b, start : start + size].astype(F32)
        for j in range(size // 2):
            pair = [fx[pl.ds(2 * j + t, 8, stride=size), :] for t in range(2)]
            at = start // 2 + j
            xs[pl.ds(pl.multiple_of(zz * 16, 16), 16), at * LANES : (at + 1) * LANES] = jnp.concatenate(pair, axis=0).astype(BF16)

    def contract(w, start, size):
        cols = slice(start * LANES // 2, (start + size) * LANES // 2)
        return lax.dot_general(xs[:, cols], w[:, cols], (((1,), (1,)), ((), ())), preferred_element_type=F32)

    def expand(gate, up):
        gate = gate * factor
        hidden = (gate / (1.0 + jnp.exp(-gate)) * (up * factor)).astype(BF16)
        part[...] = jnp.dot(hidden, wd[...], preferred_element_type=F32)

    def lay_out(zz, start, size):
        for j in range(start // 2, (start + size) // 2):
            for t in range(2):
                rows = part[pl.ds(pl.multiple_of(zz * 16 + t * 8, 8), 8), j * LANES : (j + 1) * LANES]
                sums[pl.ds(zz * (NXY * PITCH) + 2 * j + t, 8, stride=PITCH), :] = rows
        for b in range(NXY):
            g = zz * NXY + b
            sb[g, start : start + size] = sums[pl.ds(pl.multiple_of(g * PITCH + start, 8), size), :].astype(BF16)

    def scatter1():
        each(0, NZ, lambda zz: lay_out(zz, 0, CUT))
        for k in NEAR[::-1]:
            send(sb.at[pl.ds(zed(k) * NXY, NXY), low], ra1.at[k], rs_send.at[1], rs1_z.at[k], dev(zed(k), xy))

    def scatter4(zz):
        lay_out(zz, CUT, ROWS - CUT)
        for k in FAR_PLANE:
            send(sb.at[zz * NXY + plane(k), high], ra4.at[zz, k - 1], rs_send.at[0], rs4_p.at[zz], dev(z, plane(k)))

    def mine_of(block, start, size):
        return sums[pl.ds(pl.multiple_of(block * PITCH + start, 8), size), :]

    def gather4(zz):
        arrive(ra4.at[zz], rs4_p.at[zz])
        total = mine_of(zz * NXY + xy, CUT, ROWS - CUT)
        for k in range(7):
            total = total + ra4[zz, k].astype(F32)

        @pl.when(z != zz)
        def _():
            k = lax.rem(zz - z + NZ, NZ)
            sb4[zz] = total.astype(BF16)
            send(sb4.at[zz], rb4.at[k], rs_send.at[2], rs4_z.at[k], dev(zz, xy))

        @pl.when(z == zz)
        def _():
            tmp[CUT:, :] = total

    def gather1():
        for k in NEAR:
            arrive(ra1.at[k], rs1_z.at[k])
        for k in (*FAR_PLANE, 0):
            p = plane(k)
            total = mine_of(z * NXY + p, 0, CUT)
            for i in NEAR:
                total = total + ra1[i, p].astype(F32)
            if k:
                sb1[k] = total.astype(BF16)
                send(sb1.at[k], rb1.at[k], rs_send.at[3], rs1_p.at[k], dev(z, p))
            else:
                tmp[:CUT, :] = total

    def collect1(zz):
        arrive_if(z != zz, rx.at[pl.ds(0, NXY), low], ag1_z.at[lax.rem(z - zz + NZ, NZ)])
        collect(zz, 0, CUT)

    def collect4(zz):
        arrive(rx.at[pl.ds(0, 7), high], ag4_p.at[zz])
        collect(zz, CUT, ROWS - CUT)

    each(0, NZ, collect1)
    for k in FAR_PLANE:
        arrive(pk_plane.at[k], pk_pr.at[k])
        peak = jnp.maximum(peak, pk_plane[k])
    pk_mine[2] = peak
    send(pk_mine.at[2], pk_both.at[0], pk_send.at[2], pk_sib, sibling)
    each(0, NZ, collect4)

    for i, (src, dst) in enumerate(own[:2]):
        pltpu.make_async_copy(src, dst.at[pl.ds(0, UNITS)], load_sem.at[i]).wait()
        arrive(dst.at[pl.ds(UNITS, UNITS)], wrecv.at[i])
    gate = contract(wg, 0, ROWS)
    up = contract(wu, 0, ROWS)
    pltpu.make_async_copy(wd_ref, wd.at[pl.ds(0, UNITS)], load_sem.at[2]).wait()
    arrive(wd.at[pl.ds(UNITS, UNITS)], wrecv.at[2])
    arrive(pk_both.at[0], pk_sib)
    top = jnp.max(jnp.maximum(peak, pk_both[0]), keepdims=True)
    factor = TARGET / (top + EPSILON)
    expand(gate, up)

    scatter1()
    each(0, NZ, scatter4)

    each(0, HALF, gather4)
    pl.when(early)(gather1)
    each(HALF, NZ, gather4)
    pl.when(z >= HALF)(gather1)

    for k in NEAR:
        arrive(rb4.at[k], rs4_z.at[k])
        tmp[CUT:, :] += rb4[k].astype(F32)
    for k in FAR_PLANE:
        arrive(rb1.at[k], rs1_p.at[k])
        tmp[:CUT, :] += rb1[k].astype(F32)
    for j in range(NJ):
        o_ref[:, j * LANES : (j + 1) * LANES] = tmp[2 * j : 2 * j + 2, :].astype(BF16)

    for i, (src, dst) in enumerate(own):
        arrive(dst.at[pl.ds(UNITS, UNITS)], wsend.at[i])
    arrive(pk_z.at[pl.ds(0, 7)], pk_send.at[0])
    arrive(pk_plane.at[pl.ds(0, 7)], pk_send.at[1])
    arrive(pk_both.at[0], pk_send.at[2])
    arrive(rx.at[pl.ds(0, 7), high], ag_send.at[0])
    arrive(rx.at[pl.ds(0, 7), low], ag_send.at[1])
    arrive(rx.at[pl.ds(0, 56), high], ag_send.at[2])
    arrive(rx.at[pl.ds(0, 56), low], ag_send.at[3])
    arrive(sb.at[pl.ds(0, 56), high], rs_send.at[0])
    arrive(sb.at[pl.ds(0, 56), low], rs_send.at[1])
    arrive(sb.at[pl.ds(0, 7), high], rs_send.at[2])
    arrive(sb.at[pl.ds(0, 7), low], rs_send.at[3])


def shards(tokens, gate_weight, up_weight, down_weight):
    vmem, hbm = pl.BlockSpec(memory_space=pltpu.VMEM), pl.BlockSpec(memory_space=pl.ANY)
    dma = pltpu.SemaphoreType.DMA
    high = ROWS - CUT
    return pl.pallas_call(
        kernel,
        out_shape=jax.ShapeDtypeStruct((2, D), BF16),
        in_specs=[hbm, hbm, hbm, hbm],
        out_specs=vmem,
        scratch_shapes=[
            pltpu.VMEM((2, D), BF16),
            pltpu.VMEM((CHIPS, ROWS, LANES), BF16),
            pltpu.VMEM((NXY * ROWS, LANES), F32),
            pltpu.VMEM((2 * CHIPS, D), BF16),
            pltpu.VMEM((2 * UNITS, D), BF16),
            pltpu.VMEM((2 * UNITS, D), BF16),
            pltpu.VMEM((2 * UNITS, D), BF16),
            pltpu.VMEM((2 * CHIPS, D), F32),
            pltpu.VMEM((CHIPS * PITCH, LANES), F32),
            pltpu.VMEM((CHIPS, ROWS, LANES), BF16),
            pltpu.VMEM((NZ, 7, high, LANES), BF16),
            pltpu.VMEM((8, NXY, CUT, LANES), BF16),
            pltpu.VMEM((8, high, LANES), BF16),
            pltpu.VMEM((8, CUT, LANES), BF16),
            pltpu.VMEM((8, high, LANES), BF16),
            pltpu.VMEM((8, CUT, LANES), BF16),
            pltpu.VMEM((ROWS, LANES), F32),
            pltpu.VMEM((3, 1, LANES), F32),
            pltpu.VMEM((8, 1, LANES), F32),
            pltpu.VMEM((8, 1, LANES), F32),
            pltpu.VMEM((1, 1, LANES), F32),
            dma, dma((3,)), dma((3,)), dma((3,)), dma((3,)), dma((8,)), dma((8,)), dma,
            pltpu.SemaphoreType.REGULAR,
            dma((4,)), dma((8,)), dma((8,)), dma((8,)), dma((8,)),
            dma((4,)), dma((8,)), dma((8,)), dma((8,)), dma((8,)),
        ],
        compiler_params=pltpu.CompilerParams(collective_id=0, has_side_effects=True, vmem_limit_bytes=60 << 20),
        name="ffn",
    )(tokens, gate_weight, up_weight, down_weight)


def solution(mesh):
    placed = (P(("dp", "tensor"), None), P("tensor", None), P("tensor", None), P("tensor", None))
    return jax.shard_map(
        shards, mesh=mesh, in_specs=placed, out_specs=P(("dp", "tensor"), None), check_vma=False
    )
```

```python
import jax
import jax.numpy as jnp
from jax import lax
from jax.experimental import pallas as pl
from jax.experimental.pallas import tpu as pltpu
from jax.sharding import PartitionSpec as P

TARGET = 16.0
EPSILON = 1e-06
F32, BF16 = jnp.float32, jnp.bfloat16

D = 4096
UNITS = 208
NZ, NX, NY = 8, 4, 2
NXY = NX * NY
CHIPS = NZ * NXY
LANES = 128
NJ = D // LANES
ROWS = 2 * NJ
PITCH = ROWS + 8
CUT = 16
NEAR = (1, 7, 2, 6, 3, 5, 4)
FAR_PLANE = (6, 5, 7, 2, 4, 1, 3)
HALF = NZ // 2


def kernel(
    x_ref, wg_ref, wu_ref, wd_ref, o_ref,
    x_in, rx, fx, xs, wg, wu, wd, part, sums, sb, ra4, ra1, sb4, sb1, rb4, rb1, tmp, pk_mine, pk_z, pk_plane, pk_both,
    x_sem, load_sem, wsend, wrecv, pk_send, pk_zr, pk_pr, pk_sib,
    here_sib, ag_send, ag4_z, ag1_p, ag4_p, ag1_z,
    rs_send, rs4_p, rs1_z, rs4_z, rs1_p,
):
    me = lax.axis_index("tensor")
    core = lax.rem(me, 2)
    chip = me // 2
    z, xy = chip // NXY, lax.rem(chip, NXY)
    y, x = xy // NX, lax.rem(xy, NX)

    def plane(k):
        return lax.rem(y + k // NX, NY) * NX + lax.rem(x + lax.rem(k, NX), NX)

    def zed(k):
        return lax.rem(z + k, NZ)

    def dev(zz, pp):
        return {"tensor": (zz * NXY + pp) * 2 + core}

    sibling = {"tensor": chip * 2 + 1 - core}

    def send(src, dst, ssem, rsem, to):
        pltpu.make_async_remote_copy(src, dst, ssem, rsem, device_id=to, device_id_type=pl.DeviceIdType.MESH).start()

    def arrive(ref, sem):
        pltpu.make_async_copy(ref, ref, sem).wait()

    barrier = pltpu.get_barrier_semaphore()

    def greet(k, _):
        pl.semaphore_signal(barrier, inc=1, device_id=dev(zed(k), xy), device_id_type=pl.DeviceIdType.MESH)
        pl.semaphore_signal(barrier, inc=1, device_id=dev(z, plane(k)), device_id_type=pl.DeviceIdType.MESH)
        return 0

    lax.fori_loop(1, 8, greet, 0)
    @pl.when(core == 0)
    def _():
        pl.semaphore_signal(barrier, inc=1, device_id=sibling, device_id_type=pl.DeviceIdType.MESH)

    x_copy = pltpu.make_async_copy(x_ref, x_in, x_sem)
    x_copy.start()
    own = [(wg_ref, wg), (wu_ref, wu), (wd_ref, wd)]
    for i, (src, dst) in enumerate(own):
        pltpu.make_async_copy(src, dst.at[pl.ds(0, UNITS)], load_sem.at[i]).start()

    x_copy.wait()
    mine = x_in[...].astype(F32)
    for j in range(NJ):
        tmp[2 * j : 2 * j + 2, :] = mine[:, j * LANES : (j + 1) * LANES]
    rx[chip] = tmp[...].astype(BF16)
    pk_mine[0] = jnp.max(jnp.abs(tmp[...]), axis=0, keepdims=True)

    pl.semaphore_wait(barrier, 14 + core)

    @pl.when(core == 1)
    def _():
        pl.semaphore_signal(here_sib, inc=1, device_id=sibling, device_id_type=pl.DeviceIdType.MESH)

    low, high = pl.ds(0, CUT), pl.ds(CUT, ROWS - CUT)

    def arrive_if(here, ref, sem):
        pl.when(here)(lambda: arrive(ref, sem))

    for k in NEAR:
        send(pk_mine.at[0], pk_z.at[k], pk_send.at[0], pk_zr.at[k], dev(zed(k), xy))
    for k in NEAR:
        send(rx.at[chip, high], rx.at[chip, high], ag_send.at[0], ag4_z.at[k], dev(zed(k), xy))
    for k in FAR_PLANE:
        send(rx.at[chip, low], rx.at[chip, low], ag_send.at[1], ag1_p.at[k], dev(z, plane(k)))

    def to_plane(zz):
        block = zz * NXY + xy
        for k in FAR_PLANE:
            send(rx.at[block, high], rx.at[block, high], ag_send.at[2], ag4_p.at[zz], dev(z, plane(k)))

    def spread4(zz):
        arrive(rx.at[zz * NXY + xy, high], ag4_z.at[lax.rem(z - zz + NZ, NZ)])
        to_plane(zz)

    def spread1(p):
        block = z * NXY + plane(p)
        if p:
            arrive(rx.at[block, low], ag1_p.at[(NX - p) % NX + p // NX * NX])
        for k in NEAR[::-1]:
            send(rx.at[block, low], rx.at[block, low], ag_send.at[3], ag1_z.at[k], dev(zed(k), xy))

    early = z < HALF
    to_plane(z)
    def weights_to_sibling():
        for i, (src, dst) in enumerate(own):
            send(src, dst.at[pl.ds(UNITS, UNITS)], wsend.at[i], wrecv.at[i], sibling)

    pl.when(core == 1)(weights_to_sibling)
    for k in (1, 7):
        spread4(zed(k))

    @pl.when(core == 0)
    def _():
        pl.semaphore_wait(here_sib, 1)
        weights_to_sibling()

    for p in range(1, 8):
        arrive(rx.at[0, low], ag1_p.at[p])
    for k in NEAR[::-1]:
        blocks = rx.at[pl.ds(z * NXY, NXY), low]
        send(blocks, blocks, ag_send.at[3], ag1_z.at[k], dev(zed(k), xy))
    for k in (2, 6):
        spread4(zed(k))
    for k in (3, 5, 4):
        spread4(zed(k))

    peak = pk_mine[0]
    for k in NEAR:
        arrive(pk_z.at[k], pk_zr.at[k])
        peak = jnp.maximum(peak, pk_z[k])
    pk_mine[1] = peak
    for k in FAR_PLANE:
        send(pk_mine.at[1], pk_plane.at[k], pk_send.at[1], pk_pr.at[k], dev(z, plane(k)))

    def collect(zz, start, size):
        for b in range(NXY):
            fx[b * size : (b + 1) * size, :] = rx[zz * NXY + b, start : start + size].astype(F32)
        for j in range(size // 2):
            pair = [fx[pl.ds(2 * j + t, 8, stride=size), :] for t in range(2)]
            at = start // 2 + j
            xs[zz * 16 : (zz + 1) * 16, at * LANES : (at + 1) * LANES] = jnp.concatenate(pair, axis=0).astype(BF16)

    def contract(w, start, size):
        cols = slice(start * LANES // 2, (start + size) * LANES // 2)
        return lax.dot_general(xs[:, cols], w[:, cols], (((1,), (1,)), ((), ())), preferred_element_type=F32)

    def expand(gate, up):
        gate = gate * factor
        hidden = (gate / (1.0 + jnp.exp(-gate)) * (up * factor)).astype(BF16)
        part[...] = jnp.dot(hidden, wd[...], preferred_element_type=F32)

    def lay_out(zz, start, size):
        for j in range(start // 2, (start + size) // 2):
            for t in range(2):
                rows = part[zz * 16 + t * 8 : zz * 16 + t * 8 + 8, j * LANES : (j + 1) * LANES]
                sums[pl.ds(zz * (NXY * PITCH) + 2 * j + t, 8, stride=PITCH), :] = rows
        for b in range(NXY):
            g = zz * NXY + b
            sb[g, start : start + size] = sums[g * PITCH + start : g * PITCH + start + size, :].astype(BF16)

    def scatter1():
        for zz in range(NZ):
            lay_out(zz, 0, CUT)
        for k in NEAR[::-1]:
            send(sb.at[pl.ds(zed(k) * NXY, NXY), low], ra1.at[k], rs_send.at[1], rs1_z.at[k], dev(zed(k), xy))

    def scatter4(zz):
        lay_out(zz, CUT, ROWS - CUT)
        for k in FAR_PLANE:
            send(sb.at[zz * NXY + plane(k), high], ra4.at[zz, k - 1], rs_send.at[0], rs4_p.at[zz], dev(z, plane(k)))

    def mine_of(block, start, size):
        return sums[pl.ds(pl.multiple_of(block * PITCH + start, 8), size), :]

    def gather4(zz):
        arrive(ra4.at[zz], rs4_p.at[zz])
        total = mine_of(zz * NXY + xy, CUT, ROWS - CUT)
        for k in range(7):
            total = total + ra4[zz, k].astype(F32)

        @pl.when(z != zz)
        def _():
            k = lax.rem(zz - z + NZ, NZ)
            sb4[zz] = total.astype(BF16)
            send(sb4.at[zz], rb4.at[k], rs_send.at[2], rs4_z.at[k], dev(zz, xy))

        @pl.when(z == zz)
        def _():
            tmp[CUT:, :] = total

    def gather1():
        for k in NEAR:
            arrive(ra1.at[k], rs1_z.at[k])
        for k in (*FAR_PLANE, 0):
            p = plane(k)
            total = mine_of(z * NXY + p, 0, CUT)
            for i in NEAR:
                total = total + ra1[i, p].astype(F32)
            if k:
                sb1[k] = total.astype(BF16)
                send(sb1.at[k], rb1.at[k], rs_send.at[3], rs1_p.at[k], dev(z, p))
            else:
                tmp[:CUT, :] = total

    for zz in range(NZ):
        arrive_if(z != zz, rx.at[pl.ds(0, NXY), low], ag1_z.at[lax.rem(z - zz + NZ, NZ)])
        collect(zz, 0, CUT)
    for k in FAR_PLANE:
        arrive(pk_plane.at[k], pk_pr.at[k])
        peak = jnp.maximum(peak, pk_plane[k])
    pk_mine[2] = peak
    send(pk_mine.at[2], pk_both.at[0], pk_send.at[2], pk_sib, sibling)
    for zz in range(NZ):
        arrive(rx.at[pl.ds(0, 7), high], ag4_p.at[zz])
        collect(zz, CUT, ROWS - CUT)

    for i, (src, dst) in enumerate(own[:2]):
        pltpu.make_async_copy(src, dst.at[pl.ds(0, UNITS)], load_sem.at[i]).wait()
        arrive(dst.at[pl.ds(UNITS, UNITS)], wrecv.at[i])
    gate = contract(wg, 0, ROWS)
    up = contract(wu, 0, ROWS)
    pltpu.make_async_copy(wd_ref, wd.at[pl.ds(0, UNITS)], load_sem.at[2]).wait()
    arrive(wd.at[pl.ds(UNITS, UNITS)], wrecv.at[2])
    arrive(pk_both.at[0], pk_sib)
    top = jnp.max(jnp.maximum(peak, pk_both[0]), keepdims=True)
    factor = TARGET / (top + EPSILON)
    expand(gate, up)

    scatter1()
    for zz in range(NZ):
        scatter4(zz)

    for zz in range(HALF):
        gather4(zz)
    pl.when(early)(gather1)
    for zz in range(HALF, NZ):
        gather4(zz)
    pl.when(z >= HALF)(gather1)

    for k in NEAR:
        arrive(rb4.at[k], rs4_z.at[k])
        tmp[CUT:, :] += rb4[k].astype(F32)
    for k in FAR_PLANE:
        arrive(rb1.at[k], rs1_p.at[k])
        tmp[:CUT, :] += rb1[k].astype(F32)
    for j in range(NJ):
        o_ref[:, j * LANES : (j + 1) * LANES] = tmp[2 * j : 2 * j + 2, :].astype(BF16)

    for i, (src, dst) in enumerate(own):
        arrive(dst.at[pl.ds(UNITS, UNITS)], wsend.at[i])
    arrive(pk_z.at[pl.ds(0, 7)], pk_send.at[0])
    arrive(pk_plane.at[pl.ds(0, 7)], pk_send.at[1])
    arrive(pk_both.at[0], pk_send.at[2])
    arrive(rx.at[pl.ds(0, 7), high], ag_send.at[0])
    arrive(rx.at[pl.ds(0, 7), low], ag_send.at[1])
    arrive(rx.at[pl.ds(0, 56), high], ag_send.at[2])
    arrive(rx.at[pl.ds(0, 56), low], ag_send.at[3])
    arrive(sb.at[pl.ds(0, 56), high], rs_send.at[0])
    arrive(sb.at[pl.ds(0, 56), low], rs_send.at[1])
    arrive(sb.at[pl.ds(0, 7), high], rs_send.at[2])
    arrive(sb.at[pl.ds(0, 7), low], rs_send.at[3])


def shards(tokens, gate_weight, up_weight, down_weight):
    vmem, hbm = pl.BlockSpec(memory_space=pltpu.VMEM), pl.BlockSpec(memory_space=pl.ANY)
    dma = pltpu.SemaphoreType.DMA
    high = ROWS - CUT
    return pl.pallas_call(
        kernel,
        out_shape=jax.ShapeDtypeStruct((2, D), BF16),
        in_specs=[hbm, hbm, hbm, hbm],
        out_specs=vmem,
        scratch_shapes=[
            pltpu.VMEM((2, D), BF16),
            pltpu.VMEM((CHIPS, ROWS, LANES), BF16),
            pltpu.VMEM((NXY * ROWS, LANES), F32),
            pltpu.VMEM((2 * CHIPS, D), BF16),
            pltpu.VMEM((2 * UNITS, D), BF16),
            pltpu.VMEM((2 * UNITS, D), BF16),
            pltpu.VMEM((2 * UNITS, D), BF16),
            pltpu.VMEM((2 * CHIPS, D), F32),
            pltpu.VMEM((CHIPS * PITCH, LANES), F32),
            pltpu.VMEM((CHIPS, ROWS, LANES), BF16),
            pltpu.VMEM((NZ, 7, high, LANES), BF16),
            pltpu.VMEM((8, NXY, CUT, LANES), BF16),
            pltpu.VMEM((8, high, LANES), BF16),
            pltpu.VMEM((8, CUT, LANES), BF16),
            pltpu.VMEM((8, high, LANES), BF16),
            pltpu.VMEM((8, CUT, LANES), BF16),
            pltpu.VMEM((ROWS, LANES), F32),
            pltpu.VMEM((3, 1, LANES), F32),
            pltpu.VMEM((8, 1, LANES), F32),
            pltpu.VMEM((8, 1, LANES), F32),
            pltpu.VMEM((1, 1, LANES), F32),
            dma, dma((3,)), dma((3,)), dma((3,)), dma((3,)), dma((8,)), dma((8,)), dma,
            pltpu.SemaphoreType.REGULAR,
            dma((4,)), dma((8,)), dma((8,)), dma((8,)), dma((8,)),
            dma((4,)), dma((8,)), dma((8,)), dma((8,)), dma((8,)),
        ],
        compiler_params=pltpu.CompilerParams(collective_id=0, has_side_effects=True, vmem_limit_bytes=60 << 20),
        name="ffn",
    )(tokens, gate_weight, up_weight, down_weight)


def solution(mesh):
    placed = (P(("dp", "tensor"), None), P("tensor", None), P("tensor", None), P("tensor", None))
    return jax.shard_map(
        shards, mesh=mesh, in_specs=placed, out_specs=P(("dp", "tensor"), None), check_vma=False
    )
```
